256 devices in a mesh: dp: 8 (over z), vocab: 32 (over x, y, core).
Axes of the slice: x: 4, y: 4, z: 8, core: 2. Of those that a mesh axis runs over, the one named last changes fastest.
Arguments:
- hidden: bfloat16 [768, 5120], P('dp', 'vocab'), may hold values from -64 to 64
- head_weight: bfloat16 [5120, 151552], P(None, ('dp', 'vocab')), may hold values from -3 to 3
- targets: int32 [768], P('dp'), may hold values from 0 to 151551
- advantage: float32 [768], P('dp'), may hold values from -4 to 4
- policy_mask: int32 [768], P('dp'), may hold values from 0 to 1, as said below
Outputs:
- hidden_grad: bfloat16 [768, 5120], P('dp', 'vocab')
- head_grad: bfloat16 [5120, 151552], P(None, ('dp', 'vocab'))
- loss: float32 [], replicated
The draws below stay inside these ranges and needn't reach their ends.
Inputs may be any that keep to these rules, and one draw needn't show every extreme that they name: `policy_mask`: exactly 384 tokens are marked 1 in all, and the 96 tokens of one index of dp are all marked.
All inputs are finite; a program needn't handle non-finite values.
Results may differ from the reference program's by a relative error of at most 0.012.
Values may be sent and summed in bfloat16 or wider, within the bound.
No kernel may reach another device: no remote copies, remote signals or barrier semaphores. Data moves between devices by JAX's collectives and lax.ppermute only.
A program may use at most 128 MiB of HBM per device.

```python
import math
import jax
import jax.numpy as jnp
import numpy as np
from jax import lax

D = 5120
VOCAB = 151552
TOK_DEV = 96
TOKENS = 768
POLICY = 384
N_DP = 8
N_VOCAB = 32


def draw_hidden(key, part):
    key = jax.random.fold_in(key, 5)
    key_base, key_scale = jax.random.split(key, 2)
    base = jnp.clip(jax.random.normal(key_base, (TOKENS, D), jnp.float32), -4.0, 4.0)
    row_scale = jnp.exp(jax.random.uniform(key_scale, (TOKENS, 1), jnp.float32, math.log(0.3), math.log(10.0)))
    return (base * row_scale).astype(jnp.bfloat16)


def draw_head_weight(key, part):
    key = jax.random.fold_in(key, 9)
    key_shared, key_separate = jax.random.split(key)
    weight_scale = 3.0 / math.sqrt(D)
    shared = jnp.clip(jax.random.normal(key_shared, (D, 1), jnp.float32), -4.0, 4.0)
    separate = jnp.clip(jax.random.normal(key_separate, (D, VOCAB), jnp.float32), -4.0, 4.0)
    combined = 0.6 * shared + 0.8 * separate
    return (weight_scale * combined).astype(jnp.bfloat16)


def draw_policy_mask(key, part):
    key = jax.random.fold_in(key, 7)
    key_group, key_order = jax.random.split(key)
    group_count = TOKENS // TOK_DEV
    full_group = jax.random.randint(key_group, (), 0, group_count)
    group_of = jnp.arange(TOKENS, dtype=jnp.int32) // TOK_DEV
    inside = group_of == full_group
    shuffled = jax.random.permutation(key_order, TOKENS).astype(jnp.int32)
    priority = jnp.where(inside, shuffled + TOKENS, shuffled)
    rank_all = jnp.argsort(jnp.argsort(priority, stable=True), stable=True)
    chosen = jnp.logical_or(rank_all < POLICY - TOK_DEV, inside)
    return chosen.astype(jnp.int32)


def plant(drawn, own_key, smallest, high):
    index_at = [jax.random.randint(jax.random.fold_in(own_key, axis), (), 0, length) for axis, length in enumerate(drawn.shape)]
    longest = drawn.shape.index(max(drawn.shape))
    next_to = index_at[:longest] + [(index_at[longest] + 1) % drawn.shape[longest]] + index_at[longest + 1:]
    return drawn.at[tuple(index_at)].set(smallest).at[tuple(next_to)].set(high)


def shard_levels(key, shape, cuts, least, top_value):
    level = 1.0
    for position, parts in cuts:
        steps = jax.random.uniform(jax.random.fold_in(jax.random.fold_in(key, 6), position), (parts,), jnp.float32, least / len(cuts), top_value / len(cuts))
        level = level * jnp.repeat(jnp.exp(steps), shape[position] // parts).reshape((-1,) + (1,) * (len(shape) - 1 - position))
    return level


def skewed_wide(own_key, shape, count, lean):
    loads = [min(1 << octave, count + 1 - (1 << octave)) * (1 << 20) // math.isqrt((1 << octave) ** lean) + 1 for octave in range((count + 1).bit_length()) if 1 << octave <= count]
    scale = 1 + sum(loads) // (1 << 30)
    table = np.cumsum(np.array([max(1, weight // scale) for weight in loads]))
    lot = jax.random.randint(jax.random.fold_in(own_key, 1), shape, 0, int(table[len(loads) - 1]))
    start = jnp.left_shift(1, jnp.searchsorted(jnp.asarray(table, jnp.int32), lot, side="right").astype(jnp.int32))
    standing = start - 1 + jax.random.randint(jax.random.fold_in(own_key, 4), shape, 0, 1 << 30) % jnp.minimum(start, count + 1 - start)
    return jax.random.permutation(jax.random.fold_in(own_key, 2), count)[standing].astype(jnp.int32)


def noise(stream_key, dims, spread, bound, cuts=(), kind=jnp.bfloat16):
    loudness = shard_levels(stream_key, dims, cuts, -0.22, 0.18) if cuts else 1.0
    drawn = jax.random.normal(stream_key, dims, jnp.float32) * spread * loudness
    return jnp.minimum(jnp.maximum(drawn, -bound), bound).astype(kind)


def setup_inputs(seed: int = 0) -> dict:
    arg_keys = jax.random.split(jax.random.key(seed), 6)
    hidden = draw_hidden(jax.random.fold_in(arg_keys[5], 71), 0)
    head_weight = draw_head_weight(jax.random.fold_in(arg_keys[5], 71), 0)
    targets = plant(skewed_wide(arg_keys[2], (TOKENS,), VOCAB, 2), jax.random.fold_in(arg_keys[2], 3), 0, VOCAB - 1).astype(jnp.int32)
    advantage = noise(arg_keys[3], (TOKENS,), 1.0, 4.0, ((0, 8),), jnp.float32)
    policy_mask = draw_policy_mask(jax.random.fold_in(arg_keys[5], 71), 0)
    return dict(hidden=hidden, head_weight=head_weight, targets=targets, advantage=advantage, policy_mask=policy_mask)


entropy_coef = 0.02

def reference(hidden, head_weight, targets, advantage, policy_mask):
    picked = jnp.nonzero(policy_mask > 0, size=POLICY)[0].astype(jnp.int32)
    policy_rows = hidden[picked]
    targets_kept = targets[picked]
    advantage_kept = advantage[picked]
    logits = jnp.dot(policy_rows, head_weight, preferred_element_type=jnp.float32)
    row_top = lax.optimization_barrier(jnp.max(logits, axis=1))
    shifted = jnp.exp(logits - row_top[:, None])
    row_total = lax.optimization_barrier(jnp.sum(shifted, axis=1))
    row_mix = lax.optimization_barrier(jnp.sum(shifted * logits, axis=1))
    chosen = jnp.take_along_axis(logits, targets_kept[:, None], axis=1)[:, 0]
    log_total = row_top + jnp.log(row_total)
    mean_logit = row_mix / row_total
    probs = shifted / row_total[:, None]
    columns = jnp.arange(VOCAB, dtype=jnp.int32)
    is_target = (targets_kept[:, None] == columns[None, :]).astype(jnp.float32)
    dlogits = ((advantage_kept[:, None] * (probs - is_target) + entropy_coef * probs * (logits - mean_logit[:, None])) / POLICY).astype(jnp.bfloat16)
    loss = -jnp.sum(advantage_kept * (chosen - log_total) + entropy_coef * (log_total - mean_logit)) / POLICY
    block_count = N_DP * N_VOCAB
    block_width = VOCAB // block_count
    dl_blocks = dlogits.reshape(POLICY, block_count, block_width).transpose(1, 0, 2)
    rows_left = policy_rows.T

    def block_grad(dl_block):
        return jnp.dot(rows_left, dl_block, preferred_element_type=jnp.float32).astype(jnp.bfloat16)
    head_blocks = lax.map(block_grad, dl_blocks)
    head_grad = head_blocks.transpose(1, 0, 2).reshape(D, VOCAB)

    def add_block(block_index, total):
        start = (block_index * block_width).astype(jnp.int32)
        dl_part = lax.dynamic_slice_in_dim(dlogits, start, block_width, 1)
        weight_part = lax.dynamic_slice_in_dim(head_weight, start, block_width, 1)
        partial_grad = lax.dot_general(dl_part, weight_part, (((1,), (1,)), ((), ())), preferred_element_type=jnp.float32)
        return total + partial_grad
    grad_sum = lax.fori_loop(0, block_count, add_block, jnp.zeros((POLICY, D), jnp.float32))
    grad_rows = grad_sum.astype(jnp.bfloat16)
    hidden_grad = jnp.zeros((TOKENS, D), jnp.bfloat16).at[picked].set(grad_rows)
    return (hidden_grad, head_grad, loss)
```

```python
import functools

import jax
import jax.numpy as jnp
from jax import lax
from jax.experimental import pallas as pl
from jax.experimental.pallas import tpu as pltpu
from jax.sharding import Mesh, PartitionSpec as P

entropy_coef = 0.02
tok = 96
policy = 384
width = 160
cols = 592
meta_rows = 16
bf16 = jnp.bfloat16
f32 = jnp.float32
nt_dims = (((1,), (1,)), ((), ()))
tn_dims = (((0,), (0,)), ((), ()))
vmem = pltpu.CompilerParams(vmem_limit_bytes=48 * 1024 * 1024)


def pack_kernel(hidden_ref, targets_ref, adv_ref, mask_ref, out_ref):
    adv = adv_ref[...]
    high = adv.astype(bf16).astype(f32)
    rest = adv - high
    mid = rest.astype(bf16).astype(f32)
    low = rest - mid
    targets = targets_ref[...]
    rows = [
        jnp.where(mask_ref[...] > 0, 1.0, 0.0),
        high,
        mid,
        low,
        (targets & 63).astype(f32),
        ((targets >> 6) & 63).astype(f32),
        (targets >> 12).astype(f32),
    ]
    rows.append(jnp.zeros((meta_rows - len(rows), tok), f32))
    meta = jnp.concatenate(rows, axis=0).astype(bf16)
    for z in range(out_ref.shape[0]):
        out_ref[z, :width, :] = hidden_ref[...]
        out_ref[z, width:, :] = meta


def compact_kernel(blocks_ref, rows_ref, meta_ref, rank_ref):
    groups = blocks_ref.shape[0]
    mask = jnp.concatenate(
        [blocks_ref[z, width : width + meta_rows, :].astype(f32)[:1] for z in range(groups)], axis=0
    )
    before = lax.broadcasted_iota(jnp.int32, (tok, tok), 0) < lax.broadcasted_iota(jnp.int32, (tok, tok), 1)
    prefix = jnp.dot(mask.astype(bf16), before.astype(bf16), preferred_element_type=f32)
    total = jnp.broadcast_to(jnp.sum(mask, axis=1, keepdims=True), mask.shape)
    start = jnp.zeros((1, tok), f32)
    starts = []
    for z in range(groups):
        starts.append(start)
        start = start + total[z : z + 1]
    rank = jnp.where(mask > 0, prefix + jnp.concatenate(starts, axis=0), -1.0).astype(jnp.int32)
    rank_ref[...] = rank
    place = lax.broadcasted_iota(jnp.int32, (policy, tok), 0)
    acc = jnp.zeros((width + meta_rows, policy), f32)
    for z in range(groups):
        pick = (place == rank[z : z + 1]).astype(f32).astype(bf16)
        acc += lax.dot_general(blocks_ref[z], pick, nt_dims, preferred_element_type=f32)
    meta_ref[...] = acc[width:]
    rows = acc[:width].astype(bf16)
    for other in range(rows_ref.shape[0]):
        rows_ref[other] = rows


def row_tile(core, mine, partner):
    first = jnp.where(core == 0, mine, partner)
    second = jnp.where(core == 0, partner, mine)
    pieces = []
    for block in range(mine.shape[0]):
        pieces += [first[block], second[block]]
    return jnp.concatenate(pieces, axis=0)


def meta_target(meta):
    return (meta[4:5] + 64.0 * meta[5:6] + 4096.0 * meta[6:7]).astype(jnp.int32)


def meta_advantage(meta):
    return meta[1:2] + meta[2:3] + meta[3:4]


def column_is_target(place_ref, meta):
    column = place_ref[1] + lax.broadcasted_iota(jnp.int32, (cols, policy), 0)
    return column == meta_target(meta)


def logits_kernel(place_ref, weight_ref, mine_ref, partner_ref, meta_ref, logits_ref, stats_ref):
    step = pl.program_id(0)
    tile = row_tile(place_ref[0], mine_ref[...], partner_ref[...])
    part = jnp.dot(weight_ref[...], tile, preferred_element_type=f32)

    @pl.when(step == 0)
    def _():
        logits_ref[...] = part

    @pl.when(step > 0)
    def _():
        logits_ref[...] += part

    @pl.when(step == pl.num_programs(0) - 1)
    def _():
        logits = logits_ref[...]
        top = jnp.max(logits, axis=0, keepdims=True)
        shifted = jnp.exp(logits - top)
        total = jnp.sum(shifted, axis=0, keepdims=True)
        mix = jnp.sum(shifted * logits, axis=0, keepdims=True)
        chosen = jnp.sum(
            jnp.where(column_is_target(place_ref, meta_ref[...]), logits, 0.0), axis=0, keepdims=True
        )
        stats = jnp.concatenate([top, total, mix, chosen, jnp.zeros((4, policy), f32)], axis=0)
        for other in range(stats_ref.shape[0]):
            stats_ref[other] = stats


def combine(stats):
    tops = stats[:, 0:1, :]
    top = jnp.max(tops, axis=0)
    scale = jnp.exp(tops - top[None])
    total = jnp.sum(stats[:, 1:2, :] * scale, axis=0)
    mix = jnp.sum(stats[:, 2:3, :] * scale, axis=0)
    chosen = jnp.sum(stats[:, 3:4, :], axis=0)
    return top, total, mix, chosen


def combine_kernel(in_ref, out_ref):
    top, total, mix, chosen = combine(in_ref[...])
    stats = jnp.concatenate([top, total, mix, chosen, jnp.zeros((4, policy), f32)], axis=0)
    for other in range(out_ref.shape[0]):
        out_ref[other] = stats


def grad_kernel(place_ref, stats_ref, meta_ref, logits_ref, weight_ref, grad_ref, dlogits_ref, loss_ref):
    @pl.when(pl.program_id(0) == 0)
    def _():
        top, total, mix, chosen = combine(stats_ref[...])
        meta = meta_ref[...]
        adv = meta_advantage(meta)
        mean = mix / total
        log_total = top + jnp.log(total)
        loss = jnp.sum(
            adv * (chosen - log_total) + entropy_coef * (log_total - mean), axis=1, keepdims=True
        )
        loss_ref[...] = -loss / policy
        logits = logits_ref[...]
        probs = jnp.exp(logits - top) / total
        hit = column_is_target(place_ref, meta).astype(f32)
        dlogits = (adv * (probs - hit) + entropy_coef * probs * (logits - mean)) / policy
        dlogits_ref[...] = dlogits.astype(bf16)

    tile = lax.dot_general(weight_ref[...], dlogits_ref[...], tn_dims, preferred_element_type=f32)
    tile = tile.astype(bf16)
    for block in range(grad_ref.shape[1]):
        for core in range(2):
            at = (2 * block + core) * width
            grad_ref[core, block] = tile[at : at + width]


def head_kernel(place_ref, dlogits_ref, mine_ref, partner_ref, out_ref):
    tile = row_tile(place_ref[0], mine_ref[...], partner_ref[...])
    out_ref[...] = lax.dot_general(
        dlogits_ref[...], tile, nt_dims, preferred_element_type=f32
    ).astype(bf16)


def add_kernel(mine_ref, partner_ref, out_ref):
    out_ref[...] = (mine_ref[...].astype(f32) + partner_ref[...].astype(f32)).astype(bf16)


def spread_kernel(parts_ref, rank_ref, out_ref):
    total = jnp.sum(parts_ref[...].astype(f32), axis=0).astype(bf16)
    place = lax.broadcasted_iota(jnp.int32, (policy, tok), 0)
    for z in range(out_ref.shape[0]):
        pick = (place == rank_ref[z : z + 1, :]).astype(f32).astype(bf16)
        out_ref[z] = jnp.dot(total, pick, preferred_element_type=f32).astype(bf16)


def sum_kernel(parts_ref, out_ref):
    out_ref[...] = jnp.sum(parts_ref[...].astype(f32), axis=0).astype(bf16)


def shape(*dims, dtype=bf16):
    return jax.ShapeDtypeStruct(dims, dtype)


def body(hidden, head_weight, targets, advantage, policy_mask):
    n_dp = lax.axis_size("z")
    n_plane = lax.axis_size("x") * lax.axis_size("y")
    core = lax.axis_index("c")
    device = lax.axis_index(("z", "x", "y", "c"))
    place = jnp.stack([core, device * cols]).astype(jnp.int32)
    weight = head_weight.T
    depth = weight.shape[1]
    swap = [(0, 1), (1, 0)]
    tiles = 4
    tile = depth // tiles
    blocks = n_plane // tiles

    packed = pl.pallas_call(
        pack_kernel, out_shape=shape(n_dp, width + meta_rows, tok), name="pack"
    )(hidden.T, targets[None], advantage[None], policy_mask[None])
    packed = lax.all_to_all(packed, "z", 0, 0)
    rows, meta, rank = pl.pallas_call(
        compact_kernel,
        out_shape=(
            shape(n_plane, width, policy),
            shape(meta_rows, policy, dtype=f32),
            shape(n_dp, tok, dtype=jnp.int32),
        ),
        name="compact",
    )(packed)
    mine = lax.all_to_all(rows, ("x", "y"), 0, 0)
    partner = lax.ppermute(mine, "c", swap)

    smem = pl.BlockSpec(memory_space=pltpu.SMEM)
    weight_spec = pl.BlockSpec((cols, tile), lambda i: (0, i))
    rows_spec = pl.BlockSpec((blocks, width, policy), lambda i: (i, 0, 0))

    def whole(*dims):
        return pl.BlockSpec(dims, lambda i: (0,) * len(dims))

    logits, stats = pl.pallas_call(
        logits_kernel,
        grid=(tiles,),
        in_specs=[smem, weight_spec, rows_spec, rows_spec, whole(meta_rows, policy)],
        out_specs=[whole(cols, policy), whole(2 * n_dp, 8, policy)],
        out_shape=(shape(cols, policy, dtype=f32), shape(2 * n_dp, 8, policy, dtype=f32)),
        compiler_params=vmem,
        name="logits",
    )(place, weight, mine, partner, meta)

    stats = lax.all_to_all(stats, ("z", "c"), 0, 0)
    stats = pl.pallas_call(
        combine_kernel, out_shape=shape(n_plane, 8, policy, dtype=f32), name="combine"
    )(stats)
    stats = lax.all_to_all(stats, ("x", "y"), 0, 0)

    grad, dlogits, loss = pl.pallas_call(
        grad_kernel,
        grid=(tiles,),
        in_specs=[
            smem,
            whole(n_plane, 8, policy),
            whole(meta_rows, policy),
            whole(cols, policy),
            weight_spec,
        ],
        out_specs=[
            pl.BlockSpec((2, blocks, width, policy), lambda i: (0, i, 0, 0)),
            whole(cols, policy),
            whole(1, 1),
        ],
        out_shape=(
            shape(2, n_plane, width, policy),
            shape(cols, policy),
            shape(1, 1, dtype=f32),
        ),
        compiler_params=vmem,
        name="grad",
    )(place, stats, meta, logits, weight)

    kept = lax.dynamic_index_in_dim(grad, core, 0, keepdims=False)
    sent = lax.dynamic_index_in_dim(grad, 1 - core, 0, keepdims=False)
    got = lax.ppermute(sent, "c", swap)
    head_grad = pl.pallas_call(
        head_kernel,
        grid=(tiles,),
        in_specs=[smem, whole(cols, policy), rows_spec, rows_spec],
        out_specs=weight_spec,
        out_shape=shape(cols, depth),
        compiler_params=vmem,
        cost_estimate=pl.CostEstimate(
            flops=2 * cols * depth * policy, bytes_accessed=10_000_000, transcendentals=0
        ),
        name="head",
    )(place, dlogits, mine, partner)
    summed = pl.pallas_call(
        add_kernel,
        grid=(tiles,),
        in_specs=[rows_spec, rows_spec],
        out_specs=rows_spec,
        out_shape=shape(n_plane, width, policy),
        compiler_params=vmem,
        name="pair",
    )(kept, got)
    parts = lax.all_to_all(summed, ("x", "y"), 0, 0)
    spread = pl.pallas_call(
        spread_kernel, out_shape=shape(n_dp, width, tok), compiler_params=vmem, name="spread"
    )(parts, rank)
    parts = lax.all_to_all(spread, "z", 0, 0)
    grad_rows = pl.pallas_call(sum_kernel, out_shape=shape(width, tok), name="total")(parts)
    return grad_rows.T, head_grad.T, loss[0, 0]


def solution(mesh):
    fine = Mesh(mesh.devices.reshape(8, 4, 4, 2), ("z", "x", "y", "c"))
    every = ("z", "x", "y", "c")
    in_specs = (P("z", ("x", "y", "c")), P(None, every), P("z"), P("z"), P("z"))
    out_specs = (P("z", ("x", "y", "c")), P(None, every), P())
    return jax.shard_map(body, mesh=fine, in_specs=in_specs, out_specs=out_specs, check_vma=False)
```

```python
import jax
import jax.numpy as jnp
from jax import lax
from jax.experimental import pallas as pl
from jax.experimental.pallas import tpu as pltpu
from jax.sharding import Mesh, PartitionSpec as P

entropy_coef = 0.02
tok = 96
policy = 384
width = 160
cols = 592
meta_rows = 16
bf16 = jnp.bfloat16
f32 = jnp.float32
nt_dims = (((1,), (1,)), ((), ()))
tn_dims = (((0,), (0,)), ((), ()))
small = pltpu.CompilerParams(vmem_limit_bytes=20 * 1024 * 1024)
large = pltpu.CompilerParams(vmem_limit_bytes=60 * 1024 * 1024)


def pack_kernel(hidden_ref, targets_ref, adv_ref, mask_ref, out_ref):
    adv = adv_ref[...]
    high = adv.astype(bf16).astype(f32)
    rest = adv - high
    mid = rest.astype(bf16).astype(f32)
    low = rest - mid
    targets = targets_ref[...]
    rows = [
        jnp.where(mask_ref[...] > 0, 1.0, 0.0),
        high,
        mid,
        low,
        (targets & 63).astype(f32),
        ((targets >> 6) & 63).astype(f32),
        (targets >> 12).astype(f32),
    ]
    rows.append(jnp.zeros((meta_rows - len(rows), tok), f32))
    meta = jnp.concatenate(rows, axis=0).astype(bf16)
    for z in range(out_ref.shape[0]):
        out_ref[z, :width, :] = hidden_ref[...]
        out_ref[z, width:, :] = meta


def compact_kernel(blocks_ref, rows_ref, meta_ref, rank_ref):
    groups = blocks_ref.shape[0]
    mask = jnp.concatenate(
        [blocks_ref[z, width : width + meta_rows, :].astype(f32)[:1] for z in range(groups)], axis=0
    )
    before = lax.broadcasted_iota(jnp.int32, (tok, tok), 0) < lax.broadcasted_iota(jnp.int32, (tok, tok), 1)
    prefix = jnp.dot(mask.astype(bf16), before.astype(bf16), preferred_element_type=f32)
    total = jnp.broadcast_to(jnp.sum(mask, axis=1, keepdims=True), mask.shape)
    start = jnp.zeros((1, tok), f32)
    starts = []
    for z in range(groups):
        starts.append(start)
        start = start + total[z : z + 1]
    rank = jnp.where(mask > 0, prefix + jnp.concatenate(starts, axis=0), -1.0).astype(jnp.int32)
    rank_ref[...] = rank
    place = lax.broadcasted_iota(jnp.int32, (policy, tok), 0)
    acc = jnp.zeros((width + meta_rows, policy), f32)
    for z in range(groups):
        pick = (place == rank[z : z + 1]).astype(f32).astype(bf16)
        acc += lax.dot_general(blocks_ref[z], pick, nt_dims, preferred_element_type=f32)
    meta_ref[...] = acc[width:]
    rows = acc[:width].astype(bf16)
    for other in range(rows_ref.shape[0]):
        rows_ref[other] = rows


def meta_target(meta):
    return (meta[4:5] + 64.0 * meta[5:6] + 4096.0 * meta[6:7]).astype(jnp.int32)


def meta_advantage(meta):
    return meta[1:2] + meta[2:3] + meta[3:4]


def column_is_target(place_ref, meta):
    column = place_ref[1] + lax.broadcasted_iota(jnp.int32, (cols, policy), 0)
    return column == meta_target(meta)


def prepare_kernel(place_ref, weight_ref, mine_ref, partner_ref):
    for block in range(mine_ref.shape[1] // width):
        pair = weight_ref[:, 2 * block * width : (2 * block + 2) * width]
        first, second = pair[:, :width], pair[:, width:]
        at = slice(block * width, (block + 1) * width)
        own = place_ref[0] == 0
        mine_ref[:, at] = jnp.where(own, first, second)
        partner_ref[:, at] = jnp.where(own, second, first)


def accumulate(step, out_ref, part):
    @pl.when(step == 0)
    def _():
        out_ref[...] = part

    @pl.when(step > 0)
    def _():
        out_ref[...] += part


def first_half_kernel(weight_ref, rows_ref, out_ref):
    rows = rows_ref[...].reshape(-1, policy)
    accumulate(pl.program_id(0), out_ref, jnp.dot(weight_ref[...], rows, preferred_element_type=f32))


def second_half_kernel(
    place_ref, weight_ref, rows_ref, first_ref, meta_ref, logits_ref, stats_ref
):
    step = pl.program_id(0)
    rows = rows_ref[...].reshape(-1, policy)
    accumulate(step, logits_ref, jnp.dot(weight_ref[...], rows, preferred_element_type=f32))

    @pl.when(step == pl.num_programs(0) - 1)
    def _():
        logits = logits_ref[...] + first_ref[...]
        logits_ref[...] = logits
        top = jnp.max(logits, axis=0, keepdims=True)
        shifted = jnp.exp(logits - top)
        total = jnp.sum(shifted, axis=0, keepdims=True)
        mix = jnp.sum(shifted * logits, axis=0, keepdims=True)
        chosen = jnp.sum(
            jnp.where(column_is_target(place_ref, meta_ref[...]), logits, 0.0), axis=0, keepdims=True
        )
        stats = jnp.concatenate([top, total, mix, chosen, jnp.zeros((4, policy), f32)], axis=0)
        for other in range(stats_ref.shape[0]):
            stats_ref[other] = stats


def combine(stats):
    tops = stats[:, 0:1, :]
    top = jnp.max(tops, axis=0)
    scale = jnp.exp(tops - top[None])
    total = jnp.sum(stats[:, 1:2, :] * scale, axis=0)
    mix = jnp.sum(stats[:, 2:3, :] * scale, axis=0)
    chosen = jnp.sum(stats[:, 3:4, :], axis=0)
    return top, total, mix, chosen


def combine_kernel(in_ref, out_ref):
    top, total, mix, chosen = combine(in_ref[...])
    stats = jnp.concatenate([top, total, mix, chosen, jnp.zeros((4, policy), f32)], axis=0)
    for other in range(out_ref.shape[0]):
        out_ref[other] = stats


def sent_kernel(place_ref, stats_ref, meta_ref, logits_ref, weight_ref, out_ref, dlogits_ref, loss_ref):
    @pl.when(pl.program_id(0) == 0)
    def _():
        top, total, mix, chosen = combine(stats_ref[...])
        meta = meta_ref[...]
        adv = meta_advantage(meta)
        mean = mix / total
        log_total = top + jnp.log(total)
        loss = jnp.sum(
            adv * (chosen - log_total) + entropy_coef * (log_total - mean), axis=1, keepdims=True
        )
        loss_ref[...] = -loss / policy
        logits = logits_ref[...]
        probs = jnp.exp(logits - top) / total
        hit = column_is_target(place_ref, meta).astype(f32)
        dlogits = (adv * (probs - hit) + entropy_coef * probs * (logits - mean)) / policy
        dlogits_ref[...] = dlogits.astype(bf16)

    out = lax.dot_general(weight_ref[...], dlogits_ref[...], tn_dims, preferred_element_type=f32)
    out_ref[...] = out.astype(bf16).reshape(out_ref.shape)


def kept_kernel(dlogits_ref, weight_ref, out_ref):
    out = lax.dot_general(weight_ref[...], dlogits_ref[...], tn_dims, preferred_element_type=f32)
    out_ref[...] = out.reshape(out_ref.shape)


def head_kernel(place_ref, dlogits_ref, mine_ref, partner_ref, out_ref):
    own = place_ref[0] == 0
    mine, partner = mine_ref[...], partner_ref[...]
    first = jnp.where(own, mine, partner)
    second = jnp.where(own, partner, mine)
    pieces = []
    for block in range(mine.shape[0]):
        pieces += [first[block], second[block]]
    tile = jnp.concatenate(pieces, axis=0)
    out_ref[...] = lax.dot_general(
        dlogits_ref[...], tile, nt_dims, preferred_element_type=f32
    ).astype(bf16)


def add_kernel(mine_ref, partner_ref, out_ref):
    out_ref[...] = (mine_ref[...] + partner_ref[...].astype(f32)).astype(bf16)


def spread_kernel(parts_ref, rank_ref, out_ref):
    total = jnp.sum(parts_ref[...].astype(f32), axis=0).astype(bf16)
    place = lax.broadcasted_iota(jnp.int32, (policy, tok), 0)
    for z in range(out_ref.shape[0]):
        pick = (place == rank_ref[z : z + 1, :]).astype(f32).astype(bf16)
        out_ref[z] = jnp.dot(total, pick, preferred_element_type=f32).astype(bf16)


def sum_kernel(parts_ref, out_ref):
    out_ref[...] = jnp.sum(parts_ref[...].astype(f32), axis=0).astype(bf16)


def shape(*dims, dtype=bf16):
    return jax.ShapeDtypeStruct(dims, dtype)


def cost(flops, nbytes):
    return pl.CostEstimate(flops=flops, bytes_accessed=nbytes, transcendentals=0)


def body(hidden, head_weight, targets, advantage, policy_mask):
    n_dp = lax.axis_size("z")
    n_plane = lax.axis_size("x") * lax.axis_size("y")
    core = lax.axis_index("c")
    device = lax.axis_index(("z", "x", "y", "c"))
    place = jnp.stack([core, device * cols]).astype(jnp.int32)
    weight = head_weight.T
    depth = weight.shape[1]
    half = depth // 2
    swap = [(0, 1), (1, 0)]
    tiles = 2
    blocks = n_plane // tiles
    smem = pl.BlockSpec(memory_space=pltpu.SMEM)

    def whole(*dims):
        return pl.BlockSpec(dims, lambda *i: (0,) * len(dims))

    packed = pl.pallas_call(
        pack_kernel,
        out_shape=shape(n_dp, width + meta_rows, tok),
        compiler_params=large,
        name="pack",
    )(hidden.T, targets[None], advantage[None], policy_mask[None])
    packed, weight = lax.optimization_barrier((packed, weight))
    packed = lax.all_to_all(packed, "z", 0, 0)
    weight_mine, weight_partner = pl.pallas_call(
        prepare_kernel,
        grid=(4,),
        in_specs=[smem, pl.BlockSpec((cols, depth // 4), lambda i: (0, i))],
        out_specs=[pl.BlockSpec((cols, half // 4), lambda i: (0, i))] * 2,
        out_shape=(shape(cols, half), shape(cols, half)),
        compiler_params=large,
        cost_estimate=cost(0, 24_000_000),
        name="prepare",
    )(place, weight)
    packed, weight_mine, weight_partner = lax.optimization_barrier(
        (packed, weight_mine, weight_partner)
    )
    rows, meta, rank = pl.pallas_call(
        compact_kernel,
        out_shape=(
            shape(n_plane, width, policy),
            shape(meta_rows, policy, dtype=f32),
            shape(n_dp, tok, dtype=jnp.int32),
        ),
        compiler_params=small,
        name="compact",
    )(packed)
    mine = lax.all_to_all(rows, ("x", "y"), 0, 0)
    partner = lax.ppermute(mine, "c", swap)

    rows_spec = pl.BlockSpec((blocks, width, policy), lambda i: (i, 0, 0))
    half_spec = pl.BlockSpec((cols, half // tiles), lambda i: (0, i))

    first = pl.pallas_call(
        first_half_kernel,
        grid=(tiles,),
        in_specs=[half_spec, rows_spec],
        out_specs=whole(cols, policy),
        out_shape=shape(cols, policy, dtype=f32),
        compiler_params=small,
        cost_estimate=cost(cols * depth * policy, 6_000_000),
        name="first",
    )(weight_mine, mine)
    logits, stats = pl.pallas_call(
        second_half_kernel,
        grid=(tiles,),
        in_specs=[smem, half_spec, rows_spec, whole(cols, policy), whole(meta_rows, policy)],
        out_specs=[whole(cols, policy), whole(2 * n_dp, 8, policy)],
        out_shape=(
            shape(cols, policy, dtype=f32),
            shape(2 * n_dp, 8, policy, dtype=f32),
        ),
        compiler_params=small,
        cost_estimate=cost(cols * depth * policy, 6_000_000),
        name="second",
    )(place, weight_partner, partner, first, meta)

    stats = lax.all_to_all(stats, ("z", "c"), 0, 0)
    stats = pl.pallas_call(
        combine_kernel,
        out_shape=shape(n_plane, 8, policy, dtype=f32),
        compiler_params=small,
        name="combine",
    )(stats)
    stats = lax.all_to_all(stats, ("x", "y"), 0, 0)

    sent, dlogits, loss = pl.pallas_call(
        sent_kernel,
        grid=(tiles,),
        in_specs=[
            smem,
            whole(n_plane, 8, policy),
            whole(meta_rows, policy),
            whole(cols, policy),
            half_spec,
        ],
        out_specs=[rows_spec, whole(cols, policy), whole(1, 1)],
        out_shape=(
            shape(n_plane, width, policy),
            shape(cols, policy),
            shape(1, 1, dtype=f32),
        ),
        compiler_params=small,
        cost_estimate=cost(cols * depth * policy, 6_000_000),
        name="sent",
    )(place, stats, meta, logits, weight_partner)
    got = lax.ppermute(sent, "c", swap)
    kept = pl.pallas_call(
        kept_kernel,
        grid=(tiles,),
        in_specs=[whole(cols, policy), half_spec],
        out_specs=rows_spec,
        out_shape=shape(n_plane, width, policy, dtype=f32),
        compiler_params=small,
        cost_estimate=cost(cols * depth * policy, 6_000_000),
        name="kept",
    )(dlogits, weight_mine)
    summed = pl.pallas_call(
        add_kernel,
        grid=(tiles,),
        in_specs=[rows_spec, rows_spec],
        out_specs=rows_spec,
        out_shape=shape(n_plane, width, policy),
        compiler_params=small,
        name="pair",
    )(kept, got)
    parts = lax.all_to_all(summed, ("x", "y"), 0, 0)
    spread = pl.pallas_call(
        spread_kernel, out_shape=shape(n_dp, width, tok), compiler_params=small, name="spread"
    )(parts, rank)
    spread, dlogits = lax.optimization_barrier((spread, dlogits))
    parts = lax.all_to_all(spread, "z", 0, 0)
    head_grad = pl.pallas_call(
        head_kernel,
        grid=(4,),
        in_specs=[
            smem,
            whole(cols, policy),
            pl.BlockSpec((n_plane // 4, width, policy), lambda i: (i, 0, 0)),
            pl.BlockSpec((n_plane // 4, width, policy), lambda i: (i, 0, 0)),
        ],
        out_specs=pl.BlockSpec((cols, depth // 4), lambda i: (0, i)),
        out_shape=shape(cols, depth),
        compiler_params=large,
        cost_estimate=cost(2 * cols * depth * policy, 10_000_000),
        name="head",
    )(place, dlogits, mine, partner)
    parts, head_grad = lax.optimization_barrier((parts, head_grad))
    grad_rows = pl.pallas_call(
        sum_kernel, out_shape=shape(width, tok), compiler_params=small, name="total"
    )(parts)
    return grad_rows.T, head_grad.T, loss[0, 0]


def solution(mesh):
    fine = Mesh(mesh.devices.reshape(8, 4, 4, 2), ("z", "x", "y", "c"))
    every = ("z", "x", "y", "c")
    in_specs = (P("z", ("x", "y", "c")), P(None, every), P("z"), P("z"), P("z"))
    out_specs = (P("z", ("x", "y", "c")), P(None, every), P())
    return jax.shard_map(body, mesh=fine, in_specs=in_specs, out_specs=out_specs, check_vma=False)
```

```python
import jax
import jax.numpy as jnp
from jax import lax
from jax.experimental import pallas as pl
from jax.experimental.pallas import tpu as pltpu
from jax.sharding import Mesh, PartitionSpec as P

entropy_coef = 0.02
tok = 96
policy = 384
width = 160
cols = 592
meta_rows = 16
bf16 = jnp.bfloat16
f32 = jnp.float32
nt_dims = (((1,), (1,)), ((), ()))
tn_dims = (((0,), (0,)), ((), ()))
small = pltpu.CompilerParams(vmem_limit_bytes=20 * 1024 * 1024)
large = pltpu.CompilerParams(vmem_limit_bytes=60 * 1024 * 1024)


def fold(block, corner):
    rest = [block[128:, at : at + 32] for at in (0, 32, 64)]
    return jnp.concatenate([block[:128], jnp.concatenate(rest + [corner], axis=0)], axis=1)


def unfold(folded):
    rest = [folded[at : at + 32, tok:] for at in (0, 32, 64)]
    return jnp.concatenate([folded[:, :tok], jnp.concatenate(rest, axis=1)], axis=0)


def pack_kernel(hidden_ref, targets_ref, adv_ref, mask_ref, out_ref):
    adv = adv_ref[...]
    high = adv.astype(bf16).astype(f32)
    rest = adv - high
    mid = rest.astype(bf16).astype(f32)
    low = rest - mid
    targets = targets_ref[...]
    rows = [
        jnp.where(mask_ref[...] > 0, 1.0, 0.0),
        high,
        mid,
        low,
        (targets & 63).astype(f32),
        ((targets >> 6) & 63).astype(f32),
        (targets >> 12).astype(f32),
    ]
    rows.append(jnp.zeros((1, tok), f32))
    meta = jnp.concatenate(rows, axis=0)
    pieces = [meta[:, at : at + 32] for at in (0, 32, 64)] + [jnp.zeros((8, 32), f32)]
    meta = jnp.concatenate(pieces, axis=0).astype(bf16)
    packed = fold(hidden_ref[...], meta)
    for z in range(out_ref.shape[0]):
        out_ref[z] = packed


def compact_kernel(blocks_ref, rows_ref, meta_ref, rank_ref):
    groups = blocks_ref.shape[0]
    metas = []
    for z in range(groups):
        corner = blocks_ref[z, 96:, :].astype(f32)[:, tok:]
        metas.append(jnp.concatenate([corner[at : at + 8] for at in (0, 8, 16)], axis=1))
    mask = jnp.concatenate([meta[:1] for meta in metas], axis=0)
    before = lax.broadcasted_iota(jnp.int32, (tok, tok), 0) < lax.broadcasted_iota(jnp.int32, (tok, tok), 1)
    prefix = jnp.dot(mask.astype(bf16), before.astype(bf16), preferred_element_type=f32)
    total = jnp.broadcast_to(jnp.sum(mask, axis=1, keepdims=True), mask.shape)
    start = jnp.zeros((1, tok), f32)
    starts = []
    for z in range(groups):
        starts.append(start)
        start = start + total[z : z + 1]
    rank = jnp.where(mask > 0, prefix + jnp.concatenate(starts, axis=0), -1.0).astype(jnp.int32)
    rank_ref[...] = rank
    place = lax.broadcasted_iota(jnp.int32, (policy, tok), 0)
    acc = jnp.zeros((width + meta_rows, policy), f32)
    for z in range(groups):
        pick = (place == rank[z : z + 1]).astype(f32).astype(bf16)
        meta = jnp.concatenate([metas[z], jnp.zeros_like(metas[z])], axis=0).astype(bf16)
        block = jnp.concatenate([unfold(blocks_ref[z]), meta], axis=0)
        acc += lax.dot_general(block, pick, nt_dims, preferred_element_type=f32)
    meta_ref[...] = acc[width:]
    rows = acc[:width].astype(bf16)
    for other in range(rows_ref.shape[0]):
        rows_ref[other] = rows


def meta_target(meta):
    return (meta[4:5] + 64.0 * meta[5:6] + 4096.0 * meta[6:7]).astype(jnp.int32)


def meta_advantage(meta):
    return meta[1:2] + meta[2:3] + meta[3:4]


def column_is_target(place_ref, meta):
    column = place_ref[1] + lax.broadcasted_iota(jnp.int32, (cols, policy), 0)
    return column == meta_target(meta)


def prepare_kernel(place_ref, weight_ref, kept_ref, sent_ref):
    for core, (first_ref, second_ref) in enumerate([(kept_ref, sent_ref), (sent_ref, kept_ref)]):

        @pl.when(place_ref[0] == core)
        def _():
            for block in range(kept_ref.shape[1] // width):
                at = slice(block * width, (block + 1) * width)
                first_ref[:, at] = weight_ref[:, 2 * block * width : (2 * block + 1) * width]
                second_ref[:, at] = weight_ref[:, (2 * block + 1) * width : (2 * block + 2) * width]


def accumulate(step, out_ref, part):
    @pl.when(step == 0)
    def _():
        out_ref[...] = part

    @pl.when(step > 0)
    def _():
        out_ref[...] += part


def first_half_kernel(weight_ref, rows_ref, out_ref):
    rows = rows_ref[...].reshape(-1, policy)
    accumulate(pl.program_id(0), out_ref, jnp.dot(weight_ref[...], rows, preferred_element_type=f32))


def second_half_kernel(
    place_ref, weight_ref, rows_ref, first_ref, meta_ref, logits_ref, stats_ref
):
    step = pl.program_id(0)
    rows = rows_ref[...].reshape(-1, policy)
    accumulate(step, logits_ref, jnp.dot(weight_ref[...], rows, preferred_element_type=f32))

    @pl.when(step == pl.num_programs(0) - 1)
    def _():
        logits = logits_ref[...] + first_ref[...]
        logits_ref[...] = logits
        top = jnp.max(logits, axis=0, keepdims=True)
        shifted = jnp.exp(logits - top)
        total = jnp.sum(shifted, axis=0, keepdims=True)
        mix = jnp.sum(shifted * logits, axis=0, keepdims=True)
        chosen = jnp.sum(
            jnp.where(column_is_target(place_ref, meta_ref[...]), logits, 0.0), axis=0, keepdims=True
        )
        stats = jnp.concatenate([top, total, mix, chosen], axis=0)
        for other in range(stats_ref.shape[0]):
            stats_ref[other] = stats


def combine(stats):
    tops = stats[:, 0:1, :]
    top = jnp.max(tops, axis=0)
    scale = jnp.exp(tops - top[None])
    total = jnp.sum(stats[:, 1:2, :] * scale, axis=0)
    mix = jnp.sum(stats[:, 2:3, :] * scale, axis=0)
    chosen = jnp.sum(stats[:, 3:4, :], axis=0)
    return top, total, mix, chosen


def combine_kernel(in_ref, out_ref):
    top, total, mix, chosen = combine(in_ref[...])
    stats = jnp.concatenate([top, total, mix, chosen], axis=0)
    for other in range(out_ref.shape[0]):
        out_ref[other] = stats


def dlogits_kernel(place_ref, stats_ref, meta_ref, logits_ref, dlogits_ref, loss_ref):
    top, total, mix, chosen = combine(stats_ref[...])
    meta = meta_ref[...]
    adv = meta_advantage(meta)
    mean = mix / total
    log_total = top + jnp.log(total)
    loss = jnp.sum(
        adv * (chosen - log_total) + entropy_coef * (log_total - mean), axis=1, keepdims=True
    )
    loss_ref[...] = -loss / policy
    logits = logits_ref[...]
    probs = jnp.exp(logits - top) / total
    hit = column_is_target(place_ref, meta).astype(f32)
    dlogits = (adv * (probs - hit) + entropy_coef * probs * (logits - mean)) / policy
    dlogits_ref[...] = dlogits.astype(bf16)


def grad_own_kernel(dlogits_ref, weight_ref, out_ref):
    out = lax.dot_general(weight_ref[...], dlogits_ref[...], tn_dims, preferred_element_type=f32)
    out_ref[...] = out.reshape(out_ref.shape)


def grad_sum_kernel(dlogits_ref, weight_ref, own_ref, out_ref):
    out = lax.dot_general(weight_ref[...], dlogits_ref[...], tn_dims, preferred_element_type=f32)
    out_ref[...] = (own_ref[...] + out.reshape(out_ref.shape)).astype(bf16)


def head_kernel(place_ref, dlogits_ref, mine_ref, partner_ref, out_ref):
    own = place_ref[0] == 0
    mine, partner = mine_ref[...], partner_ref[...]
    first = jnp.where(own, mine, partner)
    second = jnp.where(own, partner, mine)
    pieces = []
    for block in range(mine.shape[0]):
        pieces += [first[block], second[block]]
    tile = jnp.concatenate(pieces, axis=0)
    out_ref[...] = lax.dot_general(
        dlogits_ref[...], tile, nt_dims, preferred_element_type=f32
    ).astype(bf16)


def spread_kernel(parts_ref, rank_ref, out_ref):
    total = jnp.sum(parts_ref[...].astype(f32), axis=0).astype(bf16)
    place = lax.broadcasted_iota(jnp.int32, (policy, tok), 0)
    for z in range(out_ref.shape[0]):
        pick = (place == rank_ref[z : z + 1, :]).astype(f32).astype(bf16)
        rows = jnp.dot(total, pick, preferred_element_type=f32)
        out_ref[z] = fold(rows, jnp.zeros((32, 32), f32)).astype(bf16)


def sum_kernel(parts_ref, out_ref):
    out_ref[...] = unfold(jnp.sum(parts_ref[...].astype(f32), axis=0)).astype(bf16)


def shape(*dims, dtype=bf16):
    return jax.ShapeDtypeStruct(dims, dtype)


def cost(flops, nbytes):
    return pl.CostEstimate(flops=flops, bytes_accessed=nbytes, transcendentals=0)


def body(hidden, head_weight, targets, advantage, policy_mask):
    n_dp = lax.axis_size("z")
    n_plane = lax.axis_size("x") * lax.axis_size("y")
    core = lax.axis_index("c")
    device = lax.axis_index(("z", "x", "y", "c"))
    place = jnp.stack([core, device * cols]).astype(jnp.int32)
    weight = head_weight.T
    depth = weight.shape[1]
    half = depth // 2
    swap = [(0, 1), (1, 0)]
    tiles = 2
    blocks = n_plane // tiles
    smem = pl.BlockSpec(memory_space=pltpu.SMEM)

    def whole(*dims):
        return pl.BlockSpec(dims, lambda *i: (0,) * len(dims))

    packed = pl.pallas_call(
        pack_kernel,
        out_shape=shape(n_dp, 128, 128),
        compiler_params=large,
        name="pack",
    )(hidden.T, targets[None], advantage[None], policy_mask[None])
    packed, weight = lax.optimization_barrier((packed, weight))
    packed = lax.all_to_all(packed, "z", 0, 0)
    weight_own, weight_sent = pl.pallas_call(
        prepare_kernel,
        grid=(4,),
        in_specs=[smem, pl.BlockSpec((cols, depth // 4), lambda i: (0, i))],
        out_specs=[pl.BlockSpec((cols, half // 4), lambda i: (0, i))] * 2,
        out_shape=(shape(cols, half), shape(cols, half)),
        compiler_params=large,
        cost_estimate=cost(0, 24_000_000),
        name="prepare",
    )(place, weight)
    packed, weight_own, weight_sent = lax.optimization_barrier((packed, weight_own, weight_sent))
    rows, meta, rank = pl.pallas_call(
        compact_kernel,
        out_shape=(
            shape(n_plane, width, policy),
            shape(meta_rows, policy, dtype=f32),
            shape(n_dp, tok, dtype=jnp.int32),
        ),
        compiler_params=small,
        name="compact",
    )(packed)
    mine = lax.all_to_all(rows, ("x", "y"), 0, 0)
    partner = lax.ppermute(mine, "c", swap)

    rows_spec = pl.BlockSpec((blocks, width, policy), lambda i: (i, 0, 0))
    half_spec = pl.BlockSpec((cols, half // tiles), lambda i: (0, i))

    first = pl.pallas_call(
        first_half_kernel,
        grid=(tiles,),
        in_specs=[half_spec, rows_spec],
        out_specs=whole(cols, policy),
        out_shape=shape(cols, policy, dtype=f32),
        compiler_params=small,
        cost_estimate=cost(cols * depth * policy, 6_000_000),
        name="first",
    )(weight_own, mine)
    logits, stats = pl.pallas_call(
        second_half_kernel,
        grid=(tiles,),
        in_specs=[smem, half_spec, rows_spec, whole(cols, policy), whole(meta_rows, policy)],
        out_specs=[whole(cols, policy), whole(2 * n_dp, 4, policy)],
        out_shape=(
            shape(cols, policy, dtype=f32),
            shape(2 * n_dp, 4, policy, dtype=f32),
        ),
        compiler_params=small,
        cost_estimate=cost(cols * depth * policy, 6_000_000),
        name="second",
    )(place, weight_sent, partner, first, meta)

    logits, weight_sent = lax.optimization_barrier((logits, weight_sent))
    weight_got = lax.ppermute(weight_sent, "c", swap)
    stats = lax.all_to_all(stats, ("z", "c"), 0, 0)
    stats = pl.pallas_call(
        combine_kernel,
        out_shape=shape(n_plane, 4, policy, dtype=f32),
        compiler_params=small,
        name="combine",
    )(stats)
    stats = lax.all_to_all(stats, ("x", "y"), 0, 0)
    stats, weight_got = lax.optimization_barrier((stats, weight_got))

    dlogits, loss = pl.pallas_call(
        dlogits_kernel,
        in_specs=[smem] + [pl.BlockSpec(memory_space=pltpu.VMEM)] * 3,
        out_shape=(shape(cols, policy), shape(1, 1, dtype=f32)),
        compiler_params=small,
        name="dlogits",
    )(place, stats, meta, logits)
    dlogits_got = lax.ppermute(dlogits, "c", swap)
    grad_own = pl.pallas_call(
        grad_own_kernel,
        grid=(tiles,),
        in_specs=[whole(cols, policy), half_spec],
        out_specs=rows_spec,
        out_shape=shape(n_plane, width, policy, dtype=f32),
        compiler_params=small,
        cost_estimate=cost(cols * depth * policy, 6_000_000),
        name="grad_own",
    )(dlogits, weight_own)
    summed = pl.pallas_call(
        grad_sum_kernel,
        grid=(tiles,),
        in_specs=[whole(cols, policy), half_spec, rows_spec],
        out_specs=rows_spec,
        out_shape=shape(n_plane, width, policy),
        compiler_params=small,
        cost_estimate=cost(cols * depth * policy, 6_000_000),
        name="grad_sum",
    )(dlogits_got, weight_got, grad_own)
    parts = lax.all_to_all(summed, ("x", "y"), 0, 0)
    spread = pl.pallas_call(
        spread_kernel, out_shape=shape(n_dp, 128, 128), compiler_params=small, name="spread"
    )(parts, rank)
    spread, dlogits = lax.optimization_barrier((spread, dlogits))
    parts = lax.all_to_all(spread, "z", 0, 0)
    head_grad = pl.pallas_call(
        head_kernel,
        grid=(4,),
        in_specs=[
            smem,
            whole(cols, policy),
            pl.BlockSpec((n_plane // 4, width, policy), lambda i: (i, 0, 0)),
            pl.BlockSpec((n_plane // 4, width, policy), lambda i: (i, 0, 0)),
        ],
        out_specs=pl.BlockSpec((cols, depth // 4), lambda i: (0, i)),
        out_shape=shape(cols, depth),
        compiler_params=large,
        cost_estimate=cost(2 * cols * depth * policy, 10_000_000),
        name="head",
    )(place, dlogits, mine, partner)
    parts, head_grad = lax.optimization_barrier((parts, head_grad))
    grad_rows = pl.pallas_call(
        sum_kernel, out_shape=shape(width, tok), compiler_params=small, name="total"
    )(parts)
    return grad_rows.T, head_grad.T, loss[0, 0]


def solution(mesh):
    fine = Mesh(mesh.devices.reshape(8, 4, 4, 2), ("z", "x", "y", "c"))
    every = ("z", "x", "y", "c")
    in_specs = (P("z", ("x", "y", "c")), P(None, every), P("z"), P("z"), P("z"))
    out_specs = (P("z", ("x", "y", "c")), P(None, every), P())
    return jax.shard_map(body, mesh=fine, in_specs=in_specs, out_specs=out_specs, check_vma=False)
```

```python
import jax
import jax.numpy as jnp
from jax import lax
from jax.experimental import pallas as pl
from jax.experimental.pallas import tpu as pltpu
from jax.sharding import Mesh, PartitionSpec as P

entropy_coef = 0.02
tok = 96
policy = 384
width = 160
cols = 592
meta_rows = 16
bf16 = jnp.bfloat16
f32 = jnp.float32
nt_dims = (((1,), (1,)), ((), ()))
tn_dims = (((0,), (0,)), ((), ()))
small = pltpu.CompilerParams(vmem_limit_bytes=20 * 1024 * 1024)
large = pltpu.CompilerParams(vmem_limit_bytes=60 * 1024 * 1024)


def fold(block, corner):
    rest = [block[128:, at : at + 32] for at in (0, 32, 64)]
    return jnp.concatenate([block[:128], jnp.concatenate(rest + [corner], axis=0)], axis=1)


def unfold(folded):
    rest = [folded[at : at + 32, tok:] for at in (0, 32, 64)]
    return jnp.concatenate([folded[:, :tok], jnp.concatenate(rest, axis=1)], axis=0)


def pack_kernel(hidden_ref, targets_ref, adv_ref, mask_ref, out_ref):
    adv = adv_ref[...]
    high = adv.astype(bf16).astype(f32)
    rest = adv - high
    mid = rest.astype(bf16).astype(f32)
    low = rest - mid
    targets = targets_ref[...]
    rows = [
        jnp.where(mask_ref[...] > 0, 1.0, 0.0),
        high,
        mid,
        low,
        (targets & 63).astype(f32),
        ((targets >> 6) & 63).astype(f32),
        (targets >> 12).astype(f32),
    ]
    rows.append(jnp.zeros((1, tok), f32))
    meta = jnp.concatenate(rows, axis=0)
    pieces = [meta[:, at : at + 32] for at in (0, 32, 64)] + [jnp.zeros((8, 32), f32)]
    meta = jnp.concatenate(pieces, axis=0).astype(bf16)
    packed = fold(hidden_ref[...], meta)
    for z in range(out_ref.shape[0]):
        out_ref[z] = packed


def compact_kernel(blocks_ref, rows_ref, meta_ref, picks_ref):
    groups = blocks_ref.shape[0]
    metas = []
    for z in range(groups):
        corner = blocks_ref[z, 96:, :].astype(f32)[:, tok:]
        metas.append(jnp.concatenate([corner[at : at + 8] for at in (0, 8, 16)], axis=1))
    mask = jnp.concatenate([meta[:1] for meta in metas], axis=0)
    before = lax.broadcasted_iota(jnp.int32, (tok, tok), 0) < lax.broadcasted_iota(jnp.int32, (tok, tok), 1)
    prefix = jnp.dot(mask.astype(bf16), before.astype(bf16), preferred_element_type=f32)
    total = jnp.broadcast_to(jnp.sum(mask, axis=1, keepdims=True), mask.shape)
    start = jnp.zeros((1, tok), f32)
    starts = []
    for z in range(groups):
        starts.append(start)
        start = start + total[z : z + 1]
    rank = jnp.where(mask > 0, prefix + jnp.concatenate(starts, axis=0), -1.0).astype(jnp.int32)
    place = lax.broadcasted_iota(jnp.int32, (policy, tok), 0)
    acc = jnp.zeros((width + meta_rows, policy), f32)
    for z in range(groups):
        pick = (place == rank[z : z + 1]).astype(f32).astype(bf16)
        picks_ref[z] = pick
        meta = jnp.concatenate([metas[z], jnp.zeros_like(metas[z])], axis=0).astype(bf16)
        block = jnp.concatenate([unfold(blocks_ref[z]), meta], axis=0)
        acc += lax.dot_general(block, pick, nt_dims, preferred_element_type=f32)
    meta_ref[...] = acc[width:]
    rows = acc[:width].astype(bf16)
    for other in range(rows_ref.shape[0]):
        rows_ref[other] = rows


def meta_target(meta):
    return (meta[4:5] + 64.0 * meta[5:6] + 4096.0 * meta[6:7]).astype(jnp.int32)


def meta_advantage(meta):
    return meta[1:2] + meta[2:3] + meta[3:4]


def column_is_target(place_ref, meta):
    column = place_ref[1] + lax.broadcasted_iota(jnp.int32, (cols, policy), 0)
    return column == meta_target(meta)


def prepare_kernel(place_ref, weight_ref, kept_ref, sent_ref):
    for core, (first_ref, second_ref) in enumerate([(kept_ref, sent_ref), (sent_ref, kept_ref)]):

        @pl.when(place_ref[0] == core)
        def _():
            for block in range(kept_ref.shape[1] // width):
                at = slice(block * width, (block + 1) * width)
                first_ref[:, at] = weight_ref[:, 2 * block * width : (2 * block + 1) * width]
                second_ref[:, at] = weight_ref[:, (2 * block + 1) * width : (2 * block + 2) * width]


def first_half_kernel(weight_ref, rows_ref, out_ref):
    rows = rows_ref[...].reshape(-1, policy)
    out_ref[...] = jnp.dot(weight_ref[...], rows, preferred_element_type=f32)


def second_half_kernel(
    place_ref, weight_ref, rows_ref, first_ref, meta_ref, logits_ref, stats_ref
):
    rows = rows_ref[...].reshape(-1, policy)
    logits = first_ref[...] + jnp.dot(weight_ref[...], rows, preferred_element_type=f32)
    logits_ref[...] = logits
    top = jnp.max(logits, axis=0, keepdims=True)
    shifted = jnp.exp(logits - top)
    total = jnp.sum(shifted, axis=0, keepdims=True)
    mix = jnp.sum(shifted * logits, axis=0, keepdims=True)
    chosen = jnp.sum(
        jnp.where(column_is_target(place_ref, meta_ref[...]), logits, 0.0), axis=0, keepdims=True
    )
    stats = jnp.concatenate([top, total, mix, chosen], axis=0)
    for other in range(stats_ref.shape[0]):
        stats_ref[other] = stats


def combine(stats):
    tops = stats[:, 0:1, :]
    top = jnp.max(tops, axis=0)
    scale = jnp.exp(tops - top[None])
    total = jnp.sum(stats[:, 1:2, :] * scale, axis=0)
    mix = jnp.sum(stats[:, 2:3, :] * scale, axis=0)
    chosen = jnp.sum(stats[:, 3:4, :], axis=0)
    return top, total, mix, chosen


def combine_kernel(in_ref, out_ref):
    top, total, mix, chosen = combine(in_ref[...])
    stats = jnp.concatenate([top, total, mix, chosen], axis=0)
    for other in range(out_ref.shape[0]):
        out_ref[other] = stats


def dlogits_kernel(place_ref, stats_ref, meta_ref, logits_ref, dlogits_ref, loss_ref):
    top, total, mix, chosen = combine(stats_ref[...])
    meta = meta_ref[...]
    adv = meta_advantage(meta)
    mean = mix / total
    log_total = top + jnp.log(total)
    loss = jnp.sum(
        adv * (chosen - log_total) + entropy_coef * (log_total - mean), axis=1, keepdims=True
    )
    loss_ref[...] = -loss / policy
    logits = logits_ref[...]
    share = 1.0 / (total * policy)
    spread = entropy_coef * share
    dlogits = jnp.exp(logits - top) * (adv * share + spread * (logits - mean))
    hit = jnp.where(column_is_target(place_ref, meta), adv / policy, 0.0)
    dlogits_ref[...] = (dlogits - hit).astype(bf16)


def grad_own_kernel(dlogits_ref, weight_ref, out_ref):
    out = lax.dot_general(weight_ref[...], dlogits_ref[...], tn_dims, preferred_element_type=f32)
    out_ref[...] = out.reshape(out_ref.shape)


def grad_sum_kernel(dlogits_ref, weight_ref, own_ref, out_ref):
    out = lax.dot_general(weight_ref[...], dlogits_ref[...], tn_dims, preferred_element_type=f32)
    out_ref[...] = (own_ref[...] + out.reshape(out_ref.shape)).astype(bf16)


def head_kernel(place_ref, dlogits_ref, mine_ref, partner_ref, out_ref, rows_ref, slots_ref, sems):
    for core, (first, second) in enumerate([(mine_ref, partner_ref), (partner_ref, mine_ref)]):

        @pl.when(place_ref[0] == core)
        def _():
            for block in range(first.shape[0]):
                rows_ref[block, 0] = first[block]
                rows_ref[block, 1] = second[block]

    count = slots_ref.shape[0]
    step = slots_ref.shape[2]
    blocks = rows_ref.shape[0] // count

    def send(part):
        return pltpu.make_async_copy(
            slots_ref.at[part], out_ref.at[:, part * step : (part + 1) * step], sems.at[part]
        )

    for part in range(count):
        rows = rows_ref[part * blocks : (part + 1) * blocks].reshape(step, policy)
        slots_ref[part] = lax.dot_general(
            dlogits_ref[...], rows, nt_dims, preferred_element_type=f32
        ).astype(bf16)
        send(part).start()
    for part in range(count):
        send(part).wait()


def spread_kernel(parts_ref, picks_ref, out_ref):
    total = jnp.sum(parts_ref[...].astype(f32), axis=0).astype(bf16)
    for z in range(out_ref.shape[0]):
        rows = jnp.dot(total, picks_ref[z], preferred_element_type=f32)
        out_ref[z] = fold(rows, jnp.zeros((32, 32), f32)).astype(bf16)


def sum_kernel(parts_ref, out_ref):
    out_ref[...] = unfold(jnp.sum(parts_ref[...].astype(f32), axis=0)).astype(bf16)


def shape(*dims, dtype=bf16):
    return jax.ShapeDtypeStruct(dims, dtype)


def cost(flops, nbytes):
    return pl.CostEstimate(flops=flops, bytes_accessed=nbytes, transcendentals=0)


def body(hidden, head_weight, targets, advantage, policy_mask):
    n_dp = lax.axis_size("z")
    n_plane = lax.axis_size("x") * lax.axis_size("y")
    core = lax.axis_index("c")
    device = lax.axis_index(("z", "x", "y", "c"))
    place = jnp.stack([core, device * cols]).astype(jnp.int32)
    weight = head_weight.T
    depth = weight.shape[1]
    half = depth // 2
    swap = [(0, 1), (1, 0)]
    smem = pl.BlockSpec(memory_space=pltpu.SMEM)
    local = pl.BlockSpec(memory_space=pltpu.VMEM)

    packed = pl.pallas_call(
        pack_kernel,
        out_shape=shape(n_dp, 128, 128),
        compiler_params=large,
        name="pack",
    )(hidden.T, targets[None], advantage[None], policy_mask[None])
    packed, weight = lax.optimization_barrier((packed, weight))
    packed = lax.all_to_all(packed, "z", 0, 0)
    weight_own, weight_sent = pl.pallas_call(
        prepare_kernel,
        grid=(2,),
        in_specs=[smem, pl.BlockSpec((cols, depth // 2), lambda i: (0, i))],
        out_specs=[pl.BlockSpec((cols, half // 2), lambda i: (0, i))] * 2,
        out_shape=(shape(cols, half), shape(cols, half)),
        compiler_params=large,
        cost_estimate=cost(0, 24_000_000),
        name="prepare",
    )(place, weight)
    packed, weight_own, weight_sent = lax.optimization_barrier((packed, weight_own, weight_sent))
    rows, meta, picks = pl.pallas_call(
        compact_kernel,
        out_shape=(
            shape(n_plane, width, policy),
            shape(meta_rows, policy, dtype=f32),
            shape(n_dp, policy, tok),
        ),
        compiler_params=small,
        name="compact",
    )(packed)
    mine = lax.all_to_all(rows, ("x", "y"), 0, 0)
    partner = lax.ppermute(mine, "c", swap)

    first = pl.pallas_call(
        first_half_kernel,
        out_shape=shape(cols, policy, dtype=f32),
        compiler_params=small,
        cost_estimate=cost(cols * depth * policy, 6_000_000),
        name="first",
    )(weight_own, mine)
    logits, stats = pl.pallas_call(
        second_half_kernel,
        in_specs=[smem] + [local] * 4,
        out_shape=(
            shape(cols, policy, dtype=f32),
            shape(2 * n_dp, 4, policy, dtype=f32),
        ),
        compiler_params=small,
        cost_estimate=cost(cols * depth * policy, 6_000_000),
        name="second",
    )(place, weight_sent, partner, first, meta)

    logits, weight_sent = lax.optimization_barrier((logits, weight_sent))
    weight_got = lax.ppermute(weight_sent, "c", swap)
    stats = lax.all_to_all(stats, ("z", "c"), 0, 0)
    stats = pl.pallas_call(
        combine_kernel,
        out_shape=shape(n_plane, 4, policy, dtype=f32),
        compiler_params=small,
        name="combine",
    )(stats)
    stats = lax.all_to_all(stats, ("x", "y"), 0, 0)
    stats, weight_got = lax.optimization_barrier((stats, weight_got))

    dlogits, loss = pl.pallas_call(
        dlogits_kernel,
        in_specs=[smem] + [local] * 3,
        out_shape=(shape(cols, policy), shape(1, 1, dtype=f32)),
        compiler_params=small,
        name="dlogits",
    )(place, stats, meta, logits)
    dlogits_got = lax.ppermute(dlogits, "c", swap)
    grad_own = pl.pallas_call(
        grad_own_kernel,
        out_shape=shape(n_plane, width, policy, dtype=f32),
        compiler_params=small,
        cost_estimate=cost(cols * depth * policy, 6_000_000),
        name="grad_own",
    )(dlogits, weight_own)
    summed = pl.pallas_call(
        grad_sum_kernel,
        out_shape=shape(n_plane, width, policy),
        compiler_params=small,
        cost_estimate=cost(cols * depth * policy, 6_000_000),
        name="grad_sum",
    )(dlogits_got, weight_got, grad_own)
    parts = lax.all_to_all(summed, ("x", "y"), 0, 0)
    spread = pl.pallas_call(
        spread_kernel, out_shape=shape(n_dp, 128, 128), compiler_params=small, name="spread"
    )(parts, picks)
    spread, dlogits = lax.optimization_barrier((spread, dlogits))
    parts = lax.all_to_all(spread, "z", 0, 0)
    head_grad = pl.pallas_call(
        head_kernel,
        in_specs=[smem] + [local] * 3,
        out_specs=pl.BlockSpec(memory_space=pl.ANY),
        out_shape=shape(cols, depth),
        scratch_shapes=[
            pltpu.VMEM((n_plane, 2, width, policy), bf16),
            pltpu.VMEM((4, cols, depth // 4), bf16),
            pltpu.SemaphoreType.DMA((4,)),
        ],
        compiler_params=large,
        cost_estimate=cost(2 * cols * depth * policy, 10_000_000),
        name="head",
    )(place, dlogits, mine, partner)
    parts, head_grad = lax.optimization_barrier((parts, head_grad))
    grad_rows = pl.pallas_call(
        sum_kernel, out_shape=shape(width, tok), compiler_params=small, name="total"
    )(parts)
    return grad_rows.T, head_grad.T, loss[0, 0]


def solution(mesh):
    fine = Mesh(mesh.devices.reshape(8, 4, 4, 2), ("z", "x", "y", "c"))
    every = ("z", "x", "y", "c")
    in_specs = (P("z", ("x", "y", "c")), P(None, every), P("z"), P("z"), P("z"))
    out_specs = (P("z", ("x", "y", "c")), P(None, every), P())
    return jax.shard_map(body, mesh=fine, in_specs=in_specs, out_specs=out_specs, check_vma=False)
```

```python
import jax
import jax.numpy as jnp
from jax import lax
from jax.experimental import pallas as pl
from jax.experimental.pallas import tpu as pltpu
from jax.sharding import Mesh, PartitionSpec as P

entropy_coef = 0.02
tok = 96
policy = 384
width = 160
cols = 592
meta_rows = 16
bf16 = jnp.bfloat16
f32 = jnp.float32
nt_dims = (((1,), (1,)), ((), ()))
tn_dims = (((0,), (0,)), ((), ()))
small = pltpu.CompilerParams(vmem_limit_bytes=20 * 1024 * 1024)
large = pltpu.CompilerParams(vmem_limit_bytes=60 * 1024 * 1024)


def fold(block, corner):
    rest = [block[128:, at : at + 32] for at in (0, 32, 64)]
    return jnp.concatenate([block[:128], jnp.concatenate(rest + [corner], axis=0)], axis=1)


def unfold(folded):
    rest = [folded[at : at + 32, tok:] for at in (0, 32, 64)]
    return jnp.concatenate([folded[:, :tok], jnp.concatenate(rest, axis=1)], axis=0)


def pack_kernel(hidden_ref, targets_ref, adv_ref, mask_ref, out_ref):
    adv = adv_ref[...]
    high = adv.astype(bf16).astype(f32)
    rest = adv - high
    mid = rest.astype(bf16).astype(f32)
    low = rest - mid
    targets = targets_ref[...]
    rows = [
        jnp.where(mask_ref[...] > 0, 1.0, 0.0),
        high,
        mid,
        low,
        (targets & 63).astype(f32),
        ((targets >> 6) & 63).astype(f32),
        (targets >> 12).astype(f32),
    ]
    rows.append(jnp.zeros((1, tok), f32))
    meta = jnp.concatenate(rows, axis=0)
    pieces = [meta[:, at : at + 32] for at in (0, 32, 64)] + [jnp.zeros((8, 32), f32)]
    meta = jnp.concatenate(pieces, axis=0).astype(bf16)
    packed = fold(hidden_ref[...], meta)
    for z in range(out_ref.shape[0]):
        out_ref[z] = packed


def compact_kernel(blocks_ref, rows_ref, meta_ref, picks_ref):
    groups = blocks_ref.shape[0]
    metas = []
    for z in range(groups):
        corner = blocks_ref[z, 96:, :].astype(f32)[:, tok:]
        metas.append(jnp.concatenate([corner[at : at + 8] for at in (0, 8, 16)], axis=1))
    mask = jnp.concatenate([meta[:1] for meta in metas], axis=0)
    before = lax.broadcasted_iota(jnp.int32, (tok, tok), 0) < lax.broadcasted_iota(jnp.int32, (tok, tok), 1)
    prefix = jnp.dot(mask.astype(bf16), before.astype(bf16), preferred_element_type=f32)
    total = jnp.broadcast_to(jnp.sum(mask, axis=1, keepdims=True), mask.shape)
    start = jnp.zeros((1, tok), f32)
    starts = []
    for z in range(groups):
        starts.append(start)
        start = start + total[z : z + 1]
    rank = jnp.where(mask > 0, prefix + jnp.concatenate(starts, axis=0), -1.0).astype(jnp.int32)
    place = lax.broadcasted_iota(jnp.int32, (policy, tok), 0)
    acc = jnp.zeros((width + meta_rows, policy), f32)
    for z in range(groups):
        pick = (place == rank[z : z + 1]).astype(f32).astype(bf16)
        picks_ref[z] = pick
        meta = jnp.concatenate([metas[z], jnp.zeros_like(metas[z])], axis=0).astype(bf16)
        block = jnp.concatenate([unfold(blocks_ref[z]), meta], axis=0)
        acc += lax.dot_general(block, pick, nt_dims, preferred_element_type=f32)
    meta_ref[...] = acc[width:]
    rows = acc[:width].astype(bf16)
    for other in range(rows_ref.shape[0]):
        rows_ref[other] = rows


def meta_target(meta):
    return (meta[4:5] + 64.0 * meta[5:6] + 4096.0 * meta[6:7]).astype(jnp.int32)


def meta_advantage(meta):
    return meta[1:2] + meta[2:3] + meta[3:4]


def column_is_target(first_col, meta):
    column = first_col + lax.broadcasted_iota(jnp.int32, (cols, policy), 0)
    return column == meta_target(meta)


def prepare_kernel(place_ref, weight_ref, kept_ref, sent_ref):
    for core, (first_ref, second_ref) in enumerate([(kept_ref, sent_ref), (sent_ref, kept_ref)]):

        @pl.when(place_ref[0] == core)
        def _():
            for block in range(kept_ref.shape[1] // width):
                at = slice(block * width, (block + 1) * width)
                first_ref[:, at] = weight_ref[:, 2 * block * width : (2 * block + 1) * width]
                second_ref[:, at] = weight_ref[:, (2 * block + 1) * width : (2 * block + 2) * width]


def first_half_kernel(weight_ref, rows_ref, out_ref):
    rows = rows_ref[...].reshape(-1, policy)
    out_ref[...] = jnp.dot(weight_ref[...], rows, preferred_element_type=f32)


def second_half_kernel(
    place_ref, weight_ref, rows_ref, first_ref, meta_ref, logits_ref, stats_ref
):
    rows = rows_ref[...].reshape(-1, policy)
    logits = first_ref[...] + jnp.dot(weight_ref[...], rows, preferred_element_type=f32)
    logits_ref[...] = logits
    top = jnp.max(logits, axis=0, keepdims=True)
    shifted = jnp.exp(logits - top)
    total = jnp.sum(shifted, axis=0, keepdims=True)
    mix = jnp.sum(shifted * logits, axis=0, keepdims=True)
    chosen = jnp.sum(
        jnp.where(column_is_target(place_ref[1], meta_ref[...]), logits, 0.0), axis=0, keepdims=True
    )
    stats = jnp.concatenate([top, total, mix, chosen], axis=0)
    for other in range(stats_ref.shape[0]):
        stats_ref[other] = stats


def combine(stats):
    tops = stats[:, 0:1, :]
    top = jnp.max(tops, axis=0)
    scale = jnp.exp(tops - top[None])
    total = jnp.sum(stats[:, 1:2, :] * scale, axis=0)
    mix = jnp.sum(stats[:, 2:3, :] * scale, axis=0)
    chosen = jnp.sum(stats[:, 3:4, :], axis=0)
    return top, total, mix, chosen


def combine_kernel(in_ref, out_ref):
    top, total, mix, chosen = combine(in_ref[...])
    stats = jnp.concatenate([top, total, mix, chosen], axis=0)
    for other in range(out_ref.shape[0]):
        out_ref[other] = stats


def grad_kernel(
    place_ref, stats_ref, meta_ref, logits_ref, other_ref, weight_ref, weight_got_ref, grad_ref, dlogits_ref, loss_ref
):
    top, total, mix, chosen = combine(stats_ref[...])
    meta = meta_ref[...]
    adv = meta_advantage(meta)
    mean = mix / total
    log_total = top + jnp.log(total)
    loss = jnp.sum(
        adv * (chosen - log_total) + entropy_coef * (log_total - mean), axis=1, keepdims=True
    )
    loss_ref[...] = -loss / policy
    share = 1.0 / (total * policy)
    spread = entropy_coef * share

    def dlogits_of(logits, first_col):
        soft = jnp.exp(logits - top) * (adv * share + spread * (logits - mean))
        hit = jnp.where(column_is_target(first_col, meta), adv / policy, 0.0)
        return (soft - hit).astype(bf16)

    def part(weight, dlogits):
        return lax.dot_general(weight, dlogits, tn_dims, preferred_element_type=f32)

    whole = cols // 256 * 256
    own = dlogits_of(logits_ref[...], place_ref[1])
    dlogits_ref[...] = own
    out = part(weight_ref[:whole], own[:whole])
    other = dlogits_of(other_ref[...], place_ref[2])
    out += part(weight_got_ref[:whole], other[:whole])
    weight = jnp.concatenate([weight_ref[whole:], weight_got_ref[whole:]], axis=0)
    out += part(weight, jnp.concatenate([own[whole:], other[whole:]], axis=0))
    grad_ref[...] = out.astype(bf16).reshape(grad_ref.shape)


def head_kernel(place_ref, dlogits_ref, mine_ref, partner_ref, out_ref, rows_ref, slots_ref, sems):
    for core, (first, second) in enumerate([(mine_ref, partner_ref), (partner_ref, mine_ref)]):

        @pl.when(place_ref[0] == core)
        def _():
            for block in range(first.shape[0]):
                rows_ref[block, 0] = first[block]
                rows_ref[block, 1] = second[block]

    count = slots_ref.shape[0]
    step = slots_ref.shape[2]
    blocks = rows_ref.shape[0] // count

    def send(part):
        return pltpu.make_async_copy(
            slots_ref.at[part], out_ref.at[:, part * step : (part + 1) * step], sems.at[part]
        )

    for part in range(count):
        rows = rows_ref[part * blocks : (part + 1) * blocks].reshape(step, policy)
        slots_ref[part] = lax.dot_general(
            dlogits_ref[...], rows, nt_dims, preferred_element_type=f32
        ).astype(bf16)
        send(part).start()
    for part in range(count):
        send(part).wait()


def spread_kernel(parts_ref, picks_ref, out_ref):
    total = jnp.sum(parts_ref[...].astype(f32), axis=0).astype(bf16)
    for z in range(out_ref.shape[0]):
        rows = jnp.dot(total, picks_ref[z], preferred_element_type=f32)
        out_ref[z] = fold(rows, jnp.zeros((32, 32), f32)).astype(bf16)


def sum_kernel(parts_ref, out_ref):
    out_ref[...] = unfold(jnp.sum(parts_ref[...].astype(f32), axis=0)).astype(bf16)


def shape(*dims, dtype=bf16):
    return jax.ShapeDtypeStruct(dims, dtype)


def cost(flops, nbytes):
    return pl.CostEstimate(flops=flops, bytes_accessed=nbytes, transcendentals=0)


def body(hidden, head_weight, targets, advantage, policy_mask):
    n_dp = lax.axis_size("z")
    n_plane = lax.axis_size("x") * lax.axis_size("y")
    core = lax.axis_index("c")
    device = lax.axis_index(("z", "x", "y", "c"))
    place = jnp.stack([core, device * cols, (device + 1 - 2 * core) * cols]).astype(jnp.int32)
    weight = head_weight.T
    depth = weight.shape[1]
    half = depth // 2
    swap = [(0, 1), (1, 0)]
    smem = pl.BlockSpec(memory_space=pltpu.SMEM)
    local = pl.BlockSpec(memory_space=pltpu.VMEM)

    packed = pl.pallas_call(
        pack_kernel,
        out_shape=shape(n_dp, 128, 128),
        compiler_params=large,
        name="pack",
    )(hidden.T, targets[None], advantage[None], policy_mask[None])
    packed, weight = lax.optimization_barrier((packed, weight))
    packed = lax.all_to_all(packed, "z", 0, 0)
    weight_own, weight_sent = pl.pallas_call(
        prepare_kernel,
        grid=(2,),
        in_specs=[smem, pl.BlockSpec((cols, depth // 2), lambda i: (0, i))],
        out_specs=[pl.BlockSpec((cols, half // 2), lambda i: (0, i))] * 2,
        out_shape=(shape(cols, half), shape(cols, half)),
        compiler_params=large,
        cost_estimate=cost(0, 24_000_000),
        name="prepare",
    )(place, weight)
    packed, weight_own, weight_sent = lax.optimization_barrier((packed, weight_own, weight_sent))
    rows, meta, picks = pl.pallas_call(
        compact_kernel,
        out_shape=(
            shape(n_plane, width, policy),
            shape(meta_rows, policy, dtype=f32),
            shape(n_dp, policy, tok),
        ),
        compiler_params=small,
        name="compact",
    )(packed)
    mine = lax.all_to_all(rows, ("x", "y"), 0, 0)
    partner = lax.ppermute(mine, "c", swap)

    first = pl.pallas_call(
        first_half_kernel,
        out_shape=shape(cols, policy, dtype=f32),
        compiler_params=small,
        cost_estimate=cost(cols * depth * policy, 6_000_000),
        name="first",
    )(weight_own, mine)
    logits, stats = pl.pallas_call(
        second_half_kernel,
        in_specs=[smem] + [local] * 4,
        out_shape=(
            shape(cols, policy, dtype=f32),
            shape(2 * n_dp, 4, policy, dtype=f32),
        ),
        compiler_params=small,
        cost_estimate=cost(cols * depth * policy, 6_000_000),
        name="second",
    )(place, weight_sent, partner, first, meta)

    logits, weight_sent = lax.optimization_barrier((logits, weight_sent))
    weight_got = lax.ppermute(weight_sent, "c", swap)
    logits_got = lax.ppermute(logits, "c", swap)
    stats = lax.all_to_all(stats, ("z", "c"), 0, 0)
    stats = pl.pallas_call(
        combine_kernel,
        out_shape=shape(n_plane, 4, policy, dtype=f32),
        compiler_params=small,
        name="combine",
    )(stats)
    stats = lax.all_to_all(stats, ("x", "y"), 0, 0)
    stats, weight_got, logits_got = lax.optimization_barrier((stats, weight_got, logits_got))

    summed, dlogits, loss = pl.pallas_call(
        grad_kernel,
        in_specs=[smem] + [local] * 6,
        out_shape=(
            shape(n_plane, width, policy),
            shape(cols, policy),
            shape(1, 1, dtype=f32),
        ),
        compiler_params=small,
        cost_estimate=cost(2 * cols * depth * policy, 12_000_000),
        name="grad",
    )(place, stats, meta, logits, logits_got, weight_own, weight_got)
    parts = lax.all_to_all(summed, ("x", "y"), 0, 0)
    spread = pl.pallas_call(
        spread_kernel, out_shape=shape(n_dp, 128, 128), compiler_params=small, name="spread"
    )(parts, picks)
    spread, dlogits = lax.optimization_barrier((spread, dlogits))
    parts = lax.all_to_all(spread, "z", 0, 0)
    head_grad = pl.pallas_call(
        head_kernel,
        in_specs=[smem] + [local] * 3,
        out_specs=pl.BlockSpec(memory_space=pl.ANY),
        out_shape=shape(cols, depth),
        scratch_shapes=[
            pltpu.VMEM((n_plane, 2, width, policy), bf16),
            pltpu.VMEM((4, cols, depth // 4), bf16),
            pltpu.SemaphoreType.DMA((4,)),
        ],
        compiler_params=large,
        cost_estimate=cost(2 * cols * depth * policy, 10_000_000),
        name="head",
    )(place, dlogits, mine, partner)
    parts, head_grad = lax.optimization_barrier((parts, head_grad))
    grad_rows = pl.pallas_call(
        sum_kernel, out_shape=shape(width, tok), compiler_params=small, name="total"
    )(parts)
    return grad_rows.T, head_grad.T, loss[0, 0]


def solution(mesh):
    fine = Mesh(mesh.devices.reshape(8, 4, 4, 2), ("z", "x", "y", "c"))
    every = ("z", "x", "y", "c")
    in_specs = (P("z", ("x", "y", "c")), P(None, every), P("z"), P("z"), P("z"))
    out_specs = (P("z", ("x", "y", "c")), P(None, every), P())
    return jax.shard_map(body, mesh=fine, in_specs=in_specs, out_specs=out_specs, check_vma=False)
```

```python
import jax
import jax.numpy as jnp
from jax import lax
from jax.experimental import pallas as pl
from jax.experimental.pallas import tpu as pltpu
from jax.sharding import Mesh, PartitionSpec as P

entropy_coef = 0.02
tok = 96
policy = 384
width = 160
cols = 592
side = 4
meta_rows = 16
bf16 = jnp.bfloat16
f32 = jnp.float32
nt_dims = (((1,), (1,)), ((), ()))
tn_dims = (((0,), (0,)), ((), ()))
small = pltpu.CompilerParams(vmem_limit_bytes=20 * 1024 * 1024)
large = pltpu.CompilerParams(vmem_limit_bytes=60 * 1024 * 1024)


def fold(block, corner):
    rest = [block[128:, at : at + 32] for at in (0, 32, 64)]
    return jnp.concatenate([block[:128], jnp.concatenate(rest + [corner], axis=0)], axis=1)


def unfold(folded):
    rest = [folded[at : at + 32, tok:] for at in (0, 32, 64)]
    return jnp.concatenate([folded[:, :tok], jnp.concatenate(rest, axis=1)], axis=0)


def pack_kernel(hidden_ref, targets_ref, adv_ref, mask_ref, out_ref):
    adv = adv_ref[...]
    high = adv.astype(bf16).astype(f32)
    rest = adv - high
    mid = rest.astype(bf16).astype(f32)
    low = rest - mid
    targets = targets_ref[...]
    rows = [
        jnp.where(mask_ref[...] > 0, 1.0, 0.0),
        high,
        mid,
        low,
        (targets & 63).astype(f32),
        ((targets >> 6) & 63).astype(f32),
        (targets >> 12).astype(f32),
    ]
    rows.append(jnp.zeros((1, tok), f32))
    meta = jnp.concatenate(rows, axis=0)
    pieces = [meta[:, at : at + 32] for at in (0, 32, 64)] + [jnp.zeros((8, 32), f32)]
    meta = jnp.concatenate(pieces, axis=0).astype(bf16)
    packed = fold(hidden_ref[...], meta)
    for z in range(out_ref.shape[0]):
        out_ref[z] = packed


def compact_kernel(blocks_ref, rows_ref, meta_ref, picks_ref):
    groups = blocks_ref.shape[0]
    metas = []
    for z in range(groups):
        corner = blocks_ref[z, 96:, :].astype(f32)[:, tok:]
        metas.append(jnp.concatenate([corner[at : at + 8] for at in (0, 8, 16)], axis=1))
    mask = jnp.concatenate([meta[:1] for meta in metas], axis=0)
    before = lax.broadcasted_iota(jnp.int32, (tok, tok), 0) < lax.broadcasted_iota(jnp.int32, (tok, tok), 1)
    prefix = jnp.dot(mask.astype(bf16), before.astype(bf16), preferred_element_type=f32)
    total = jnp.broadcast_to(jnp.sum(mask, axis=1, keepdims=True), mask.shape)
    start = jnp.zeros((1, tok), f32)
    starts = []
    for z in range(groups):
        starts.append(start)
        start = start + total[z : z + 1]
    rank = jnp.where(mask > 0, prefix + jnp.concatenate(starts, axis=0), -1.0).astype(jnp.int32)
    place = lax.broadcasted_iota(jnp.int32, (policy, tok), 0)
    acc = jnp.zeros((width + meta_rows, policy), f32)
    for z in range(groups):
        pick = (place == rank[z : z + 1]).astype(f32).astype(bf16)
        picks_ref[z] = pick
        meta = jnp.concatenate([metas[z], jnp.zeros_like(metas[z])], axis=0).astype(bf16)
        block = jnp.concatenate([unfold(blocks_ref[z]), meta], axis=0)
        acc += lax.dot_general(block, pick, nt_dims, preferred_element_type=f32)
    meta_ref[...] = acc[width:]
    rows = acc[:width].astype(bf16)
    for other in range(rows_ref.shape[0]):
        rows_ref[other] = rows


def place_of(core, block):
    return jnp.where(core == 0, block, block % side * side + block // side)


def rows_of(core, rows_ref):
    return jnp.concatenate([rows_ref[place_of(core, k)] for k in range(rows_ref.shape[0])], axis=0)


def meta_target(meta):
    return (meta[4:5] + 64.0 * meta[5:6] + 4096.0 * meta[6:7]).astype(jnp.int32)


def meta_advantage(meta):
    return meta[1:2] + meta[2:3] + meta[3:4]


def column_is_target(first_col, meta):
    column = first_col + lax.broadcasted_iota(jnp.int32, (cols, policy), 0)
    return column == meta_target(meta)


def prepare_kernel(place_ref, weight_ref, kept_ref, sent_ref):
    for core, (first_ref, second_ref) in enumerate([(kept_ref, sent_ref), (sent_ref, kept_ref)]):

        @pl.when(place_ref[0] == core)
        def _():
            for block in range(kept_ref.shape[1] // width):
                at = slice(block * width, (block + 1) * width)
                first_ref[:, at] = weight_ref[:, 2 * block * width : (2 * block + 1) * width]
                second_ref[:, at] = weight_ref[:, (2 * block + 1) * width : (2 * block + 2) * width]


def first_half_kernel(place_ref, weight_ref, rows_ref, out_ref):
    rows = rows_of(place_ref[0], rows_ref)
    out_ref[...] = jnp.dot(weight_ref[...], rows, preferred_element_type=f32)


def second_half_kernel(
    place_ref, weight_ref, rows_ref, first_ref, meta_ref, logits_ref, stats_ref
):
    rows = rows_of(1 - place_ref[0], rows_ref)
    logits = first_ref[...] + jnp.dot(weight_ref[...], rows, preferred_element_type=f32)
    logits_ref[...] = logits
    top = jnp.max(logits, axis=0, keepdims=True)
    shifted = jnp.exp(logits - top)
    total = jnp.sum(shifted, axis=0, keepdims=True)
    mix = jnp.sum(shifted * logits, axis=0, keepdims=True)
    chosen = jnp.sum(
        jnp.where(column_is_target(place_ref[1], meta_ref[...]), logits, 0.0), axis=0, keepdims=True
    )
    stats = jnp.concatenate([top, total, mix, chosen], axis=0)
    for other in range(stats_ref.shape[0]):
        stats_ref[other] = stats


def combine(stats):
    tops = stats[:, 0:1, :]
    top = jnp.max(tops, axis=0)
    scale = jnp.exp(tops - top[None])
    total = jnp.sum(stats[:, 1:2, :] * scale, axis=0)
    mix = jnp.sum(stats[:, 2:3, :] * scale, axis=0)
    chosen = jnp.sum(stats[:, 3:4, :], axis=0)
    return top, total, mix, chosen


def combine_kernel(in_ref, out_ref):
    top, total, mix, chosen = combine(in_ref[...])
    stats = jnp.concatenate([top, total, mix, chosen], axis=0)
    for other in range(out_ref.shape[0]):
        out_ref[other] = stats


def grad_kernel(
    place_ref, stats_ref, meta_ref, logits_ref, other_ref, weight_ref, weight_got_ref, grad_ref, dlogits_ref, loss_ref
):
    top, total, mix, chosen = combine(stats_ref[...])
    meta = meta_ref[...]
    adv = meta_advantage(meta)
    mean = mix / total
    log_total = top + jnp.log(total)
    loss = jnp.sum(
        adv * (chosen - log_total) + entropy_coef * (log_total - mean), axis=1, keepdims=True
    )
    loss_ref[...] = -loss / policy
    share = 1.0 / (total * policy)
    spread = entropy_coef * share

    def dlogits_of(logits, first_col):
        soft = jnp.exp(logits - top) * (adv * share + spread * (logits - mean))
        hit = jnp.where(column_is_target(first_col, meta), adv / policy, 0.0)
        return (soft - hit).astype(bf16)

    def part(weight, dlogits):
        return lax.dot_general(weight, dlogits, tn_dims, preferred_element_type=f32)

    whole = cols // 256 * 256
    own = dlogits_of(logits_ref[...], place_ref[1])
    dlogits_ref[...] = own
    out = part(weight_ref[:whole], own[:whole])
    other = dlogits_of(other_ref[...], place_ref[2])
    out += part(weight_got_ref[:whole], other[:whole])
    weight = jnp.concatenate([weight_ref[whole:], weight_got_ref[whole:]], axis=0)
    out += part(weight, jnp.concatenate([own[whole:], other[whole:]], axis=0))
    for block in range(grad_ref.shape[0]):
        rows = out[block * width : (block + 1) * width]
        grad_ref[place_of(place_ref[0], block)] = rows.astype(bf16)


def head_kernel(place_ref, dlogits_ref, mine_ref, partner_ref, out_ref, rows_ref, slots_ref, sems):
    for core, (first, second) in enumerate([(mine_ref, partner_ref), (partner_ref, mine_ref)]):

        @pl.when(place_ref[0] == core)
        def _():
            for block in range(first.shape[0]):
                rows_ref[block, 0] = first[block]
                rows_ref[block, 1] = second[block % side * side + block // side]

    count = slots_ref.shape[0]
    step = slots_ref.shape[2]
    blocks = rows_ref.shape[0] // count

    def send(part):
        return pltpu.make_async_copy(
            slots_ref.at[part], out_ref.at[:, part * step : (part + 1) * step], sems.at[part]
        )

    for part in range(count):
        rows = rows_ref[part * blocks : (part + 1) * blocks].reshape(step, policy)
        slots_ref[part] = lax.dot_general(
            dlogits_ref[...], rows, nt_dims, preferred_element_type=f32
        ).astype(bf16)
        send(part).start()
    for part in range(count):
        send(part).wait()


def copies_kernel(rows_ref, out_ref):
    for other in range(out_ref.shape[0]):
        out_ref[other] = rows_ref[...]


def line_sum_kernel(parts_ref, out_ref):
    out_ref[...] = jnp.sum(parts_ref[...].astype(f32), axis=0).astype(bf16)


def spread_kernel(parts_ref, picks_ref, out_ref):
    total = jnp.sum(parts_ref[...].astype(f32), axis=0).astype(bf16)
    for z in range(out_ref.shape[0]):
        rows = jnp.dot(total, picks_ref[z], preferred_element_type=f32)
        out_ref[z] = fold(rows, jnp.zeros((32, 32), f32)).astype(bf16)


def sum_kernel(parts_ref, out_ref):
    out_ref[...] = unfold(jnp.sum(parts_ref[...].astype(f32), axis=0)).astype(bf16)


def shape(*dims, dtype=bf16):
    return jax.ShapeDtypeStruct(dims, dtype)


def along_lines(blocks, first):
    def device(x, y, c):
        return (x * side + y) * 2 + c

    near, far = (1, 0) if first else (0, 1)
    y_core, x_core = 1 - near, 1 - far
    groups = [[device(x, y, y_core) for y in range(side)] for x in range(side)]
    groups += [[device(x, y, x_core) for x in range(side)] for y in range(side)]
    return lax.all_to_all(blocks, ("x", "y", "c"), 0, 0, axis_index_groups=groups)


def cost(flops, nbytes):
    return pl.CostEstimate(flops=flops, bytes_accessed=nbytes, transcendentals=0)


def body(hidden, head_weight, targets, advantage, policy_mask):
    n_dp = lax.axis_size("z")
    n_plane = lax.axis_size("x") * lax.axis_size("y")
    core = lax.axis_index("c")
    device = lax.axis_index(("z", "x", "y", "c"))
    place = jnp.stack([core, device * cols, (device + 1 - 2 * core) * cols]).astype(jnp.int32)
    weight = head_weight.T
    depth = weight.shape[1]
    half = depth // 2
    swap = [(0, 1), (1, 0)]
    smem = pl.BlockSpec(memory_space=pltpu.SMEM)
    local = pl.BlockSpec(memory_space=pltpu.VMEM)

    packed = pl.pallas_call(
        pack_kernel,
        out_shape=shape(n_dp, 128, 128),
        compiler_params=large,
        name="pack",
    )(hidden.T, targets[None], advantage[None], policy_mask[None])
    packed, weight = lax.optimization_barrier((packed, weight))
    packed = lax.all_to_all(packed, "z", 0, 0)
    weight_own, weight_sent = pl.pallas_call(
        prepare_kernel,
        grid=(2,),
        in_specs=[smem, pl.BlockSpec((cols, depth // 2), lambda i: (0, i))],
        out_specs=[pl.BlockSpec((cols, half // 2), lambda i: (0, i))] * 2,
        out_shape=(shape(cols, half), shape(cols, half)),
        compiler_params=large,
        cost_estimate=cost(0, 24_000_000),
        name="prepare",
    )(place, weight)
    packed, weight_own, weight_sent = lax.optimization_barrier((packed, weight_own, weight_sent))
    rows, meta, picks = pl.pallas_call(
        compact_kernel,
        out_shape=(
            shape(side, width, policy),
            shape(meta_rows, policy, dtype=f32),
            shape(n_dp, policy, tok),
        ),
        compiler_params=small,
        name="compact",
    )(packed)
    line = along_lines(rows, True)
    lines = pl.pallas_call(
        copies_kernel,
        out_shape=shape(side, side, width, policy),
        compiler_params=small,
        name="copies",
    )(line)
    mine = along_lines(lines, False).reshape(n_plane, width, policy)
    partner = lax.ppermute(mine, "c", swap)

    first = pl.pallas_call(
        first_half_kernel,
        in_specs=[smem] + [local] * 2,
        out_shape=shape(cols, policy, dtype=f32),
        compiler_params=small,
        cost_estimate=cost(cols * depth * policy, 6_000_000),
        name="first",
    )(place, weight_own, mine)
    logits, stats = pl.pallas_call(
        second_half_kernel,
        in_specs=[smem] + [local] * 4,
        out_shape=(
            shape(cols, policy, dtype=f32),
            shape(2 * n_dp, 4, policy, dtype=f32),
        ),
        compiler_params=small,
        cost_estimate=cost(cols * depth * policy, 6_000_000),
        name="second",
    )(place, weight_sent, partner, first, meta)

    logits, weight_sent = lax.optimization_barrier((logits, weight_sent))
    weight_got = lax.ppermute(weight_sent, "c", swap)
    logits_got = lax.ppermute(logits, "c", swap)
    stats = lax.all_to_all(stats, ("z", "c"), 0, 0)
    stats = pl.pallas_call(
        combine_kernel,
        out_shape=shape(n_plane, 4, policy, dtype=f32),
        compiler_params=small,
        name="combine",
    )(stats)
    stats = lax.all_to_all(stats, ("x", "y"), 0, 0)
    stats, weight_got, logits_got = lax.optimization_barrier((stats, weight_got, logits_got))

    summed, dlogits, loss = pl.pallas_call(
        grad_kernel,
        in_specs=[smem] + [local] * 6,
        out_shape=(
            shape(n_plane, width, policy),
            shape(cols, policy),
            shape(1, 1, dtype=f32),
        ),
        compiler_params=small,
        cost_estimate=cost(2 * cols * depth * policy, 12_000_000),
        name="grad",
    )(place, stats, meta, logits, logits_got, weight_own, weight_got)
    parts = along_lines(summed.reshape(side, side, width, policy), False)
    line = pl.pallas_call(
        line_sum_kernel,
        out_shape=shape(side, width, policy),
        compiler_params=small,
        name="line_sum",
    )(parts)
    parts = along_lines(line, True)
    spread = pl.pallas_call(
        spread_kernel, out_shape=shape(n_dp, 128, 128), compiler_params=small, name="spread"
    )(parts, picks)
    spread, dlogits = lax.optimization_barrier((spread, dlogits))
    parts = lax.all_to_all(spread, "z", 0, 0)
    head_grad = pl.pallas_call(
        head_kernel,
        in_specs=[smem] + [local] * 3,
        out_specs=pl.BlockSpec(memory_space=pl.ANY),
        out_shape=shape(cols, depth),
        scratch_shapes=[
            pltpu.VMEM((n_plane, 2, width, policy), bf16),
            pltpu.VMEM((4, cols, depth // 4), bf16),
            pltpu.SemaphoreType.DMA((4,)),
        ],
        compiler_params=large,
        cost_estimate=cost(2 * cols * depth * policy, 10_000_000),
        name="head",
    )(place, dlogits, mine, partner)
    parts, head_grad = lax.optimization_barrier((parts, head_grad))
    grad_rows = pl.pallas_call(
        sum_kernel, out_shape=shape(width, tok), compiler_params=small, name="total"
    )(parts)
    return grad_rows.T, head_grad.T, loss[0, 0]


def solution(mesh):
    fine = Mesh(mesh.devices.reshape(8, 4, 4, 2), ("z", "x", "y", "c"))
    every = ("z", "x", "y", "c")
    in_specs = (P("z", ("x", "y", "c")), P(None, every), P("z"), P("z"), P("z"))
    out_specs = (P("z", ("x", "y", "c")), P(None, every), P())
    return jax.shard_map(body, mesh=fine, in_specs=in_specs, out_specs=out_specs, check_vma=False)
```

```python
import jax
import jax.numpy as jnp
from jax import lax
from jax.experimental import pallas as pl
from jax.experimental.pallas import tpu as pltpu
from jax.sharding import Mesh, PartitionSpec as P

entropy_coef = 0.02
tok = 96
policy = 384
width = 160
cols = 592
side = 4
meta_rows = 16
bf16 = jnp.bfloat16
f32 = jnp.float32
nt_dims = (((1,), (1,)), ((), ()))
tn_dims = (((0,), (0,)), ((), ()))
small = pltpu.CompilerParams(vmem_limit_bytes=20 * 1024 * 1024)
large = pltpu.CompilerParams(vmem_limit_bytes=60 * 1024 * 1024)


def fold(block, corner):
    rest = [block[128:, at : at + 32] for at in (0, 32, 64)]
    return jnp.concatenate([block[:128], jnp.concatenate(rest + [corner], axis=0)], axis=1)


def unfold(folded):
    rest = [folded[at : at + 32, tok:] for at in (0, 32, 64)]
    return jnp.concatenate([folded[:, :tok], jnp.concatenate(rest, axis=1)], axis=0)


def pack_kernel(hidden_ref, targets_ref, adv_ref, mask_ref, out_ref):
    adv = adv_ref[...]
    high = adv.astype(bf16).astype(f32)
    rest = adv - high
    mid = rest.astype(bf16).astype(f32)
    low = rest - mid
    targets = targets_ref[...]
    rows = [
        jnp.where(mask_ref[...] > 0, 1.0, 0.0),
        high,
        mid,
        low,
        (targets & 63).astype(f32),
        ((targets >> 6) & 63).astype(f32),
        (targets >> 12).astype(f32),
    ]
    rows.append(jnp.zeros((1, tok), f32))
    meta = jnp.concatenate(rows, axis=0)
    pieces = [meta[:, at : at + 32] for at in (0, 32, 64)] + [jnp.zeros((8, 32), f32)]
    meta = jnp.concatenate(pieces, axis=0).astype(bf16)
    packed = fold(hidden_ref[...], meta)
    for z in range(out_ref.shape[0]):
        out_ref[z] = packed


def compact_kernel(blocks_ref, rows_ref, meta_ref, picks_ref):
    groups = blocks_ref.shape[0]
    metas = []
    for z in range(groups):
        corner = blocks_ref[z, 96:, :].astype(f32)[:, tok:]
        metas.append(jnp.concatenate([corner[at : at + 8] for at in (0, 8, 16)], axis=1))
    mask = jnp.concatenate([meta[:1] for meta in metas], axis=0)
    before = lax.broadcasted_iota(jnp.int32, (tok, tok), 0) < lax.broadcasted_iota(jnp.int32, (tok, tok), 1)
    prefix = jnp.dot(mask.astype(bf16), before.astype(bf16), preferred_element_type=f32)
    total = jnp.broadcast_to(jnp.sum(mask, axis=1, keepdims=True), mask.shape)
    start = jnp.zeros((1, tok), f32)
    starts = []
    for z in range(groups):
        starts.append(start)
        start = start + total[z : z + 1]
    rank = jnp.where(mask > 0, prefix + jnp.concatenate(starts, axis=0), -1.0).astype(jnp.int32)
    place = lax.broadcasted_iota(jnp.int32, (policy, tok), 0)
    acc = jnp.zeros((width + meta_rows, policy), f32)
    for z in range(groups):
        pick = (place == rank[z : z + 1]).astype(f32).astype(bf16)
        picks_ref[z] = pick
        meta = jnp.concatenate([metas[z], jnp.zeros_like(metas[z])], axis=0).astype(bf16)
        block = jnp.concatenate([unfold(blocks_ref[z]), meta], axis=0)
        acc += lax.dot_general(block, pick, nt_dims, preferred_element_type=f32)
    meta_ref[...] = acc[width:]
    rows = acc[:width].astype(bf16)
    for other in range(rows_ref.shape[0]):
        rows_ref[other] = rows


def core_index():
    return lax.axis_index("c")


def first_column(core):
    line = lax.axis_index("z") * side + lax.axis_index("x")
    return ((line * side + lax.axis_index("y")) * 2 + core) * cols


def place_of(core, block):
    return jnp.where(core == 0, block, block % side * side + block // side)


def meta_target(meta):
    return (meta[4:5] + 64.0 * meta[5:6] + 4096.0 * meta[6:7]).astype(jnp.int32)


def meta_advantage(meta):
    return meta[1:2] + meta[2:3] + meta[3:4]


def column_is_target(first_col, meta):
    column = first_col + lax.broadcasted_iota(jnp.int32, (cols, policy), 0)
    return column == meta_target(meta)


def prepare_kernel(weight_ref, kept_ref, sent_ref):
    for core, (first_ref, second_ref) in enumerate([(kept_ref, sent_ref), (sent_ref, kept_ref)]):

        @pl.when(core_index() == core)
        def _():
            for block in range(kept_ref.shape[1] // width):
                at = slice(block * width, (block + 1) * width)
                first_ref[:, at] = weight_ref[:, 2 * block * width : (2 * block + 1) * width]
                second_ref[:, at] = weight_ref[:, (2 * block + 1) * width : (2 * block + 2) * width]


def partial_kernel(weight_ref, rows_ref, out_ref):
    @pl.when(core_index() == 0)
    def _():
        rows = rows_ref[...].reshape(-1, policy)
        out_ref[...] = jnp.dot(weight_ref[...], rows, preferred_element_type=f32)

    @pl.when(core_index() == 1)
    def _():
        blocks = [rows_ref[k % side * side + k // side] for k in range(rows_ref.shape[0])]
        rows = jnp.concatenate(blocks, axis=0)
        out_ref[...] = jnp.dot(weight_ref[...], rows, preferred_element_type=f32)


def stats_kernel(own_ref, got_ref, meta_ref, logits_ref, stats_ref):
    logits = own_ref[...] + got_ref[...]
    logits_ref[...] = logits
    top = jnp.max(logits, axis=0, keepdims=True)
    shifted = jnp.exp(logits - top)
    total = jnp.sum(shifted, axis=0, keepdims=True)
    mix = jnp.sum(shifted * logits, axis=0, keepdims=True)
    chosen = jnp.sum(
        jnp.where(column_is_target(first_column(core_index()), meta_ref[...]), logits, 0.0), axis=0, keepdims=True
    )
    stats = jnp.concatenate([top, total, mix, chosen], axis=0)
    for other in range(stats_ref.shape[0]):
        stats_ref[other] = stats


def combine(stats):
    tops = stats[:, 0:1, :]
    top = jnp.max(tops, axis=0)
    scale = jnp.exp(tops - top[None])
    total = jnp.sum(stats[:, 1:2, :] * scale, axis=0)
    mix = jnp.sum(stats[:, 2:3, :] * scale, axis=0)
    chosen = jnp.sum(stats[:, 3:4, :], axis=0)
    return top, total, mix, chosen


def combine_kernel(in_ref, out_ref):
    top, total, mix, chosen = combine(in_ref[...])
    stats = jnp.concatenate([top, total, mix, chosen], axis=0)
    for other in range(out_ref.shape[0]):
        out_ref[other] = stats


def grad_kernel(stats_ref, meta_ref, logits_ref, other_ref, weight_ref, weight_got_ref, grad_ref, dlogits_ref, loss_ref
):
    top, total, mix, chosen = combine(stats_ref[...])
    meta = meta_ref[...]
    adv = meta_advantage(meta)
    mean = mix / total
    log_total = top + jnp.log(total)
    loss = jnp.sum(
        adv * (chosen - log_total) + entropy_coef * (log_total - mean), axis=1, keepdims=True
    )
    loss_ref[...] = -loss / policy
    share = 1.0 / (total * policy)
    spread = entropy_coef * share

    def dlogits_of(logits, first_col):
        soft = jnp.exp(logits - top) * (adv * share + spread * (logits - mean))
        hit = jnp.where(column_is_target(first_col, meta), adv / policy, 0.0)
        return (soft - hit).astype(bf16)

    def part(weight, dlogits):
        return lax.dot_general(weight, dlogits, tn_dims, preferred_element_type=f32)

    whole = cols // 256 * 256
    own = dlogits_of(logits_ref[...], first_column(core_index()))
    dlogits_ref[...] = own
    out = part(weight_ref[:whole], own[:whole])
    other = dlogits_of(other_ref[...], first_column(1 - core_index()))
    out += part(weight_got_ref[:whole], other[:whole])
    weight = jnp.concatenate([weight_ref[whole:], weight_got_ref[whole:]], axis=0)
    out += part(weight, jnp.concatenate([own[whole:], other[whole:]], axis=0))
    for block in range(grad_ref.shape[0]):
        rows = out[block * width : (block + 1) * width]
        grad_ref[place_of(core_index(), block)] = rows.astype(bf16)


def head_kernel(dlogits_ref, mine_ref, partner_ref, out_ref, rows_ref, slots_ref, sems):
    for core, (first, second) in enumerate([(mine_ref, partner_ref), (partner_ref, mine_ref)]):

        @pl.when(core_index() == core)
        def _():
            for block in range(first.shape[0]):
                rows_ref[block, 0] = first[block]
                rows_ref[block, 1] = second[block % side * side + block // side]

    count = slots_ref.shape[0]
    step = slots_ref.shape[2]
    blocks = rows_ref.shape[0] // count

    def send(part):
        return pltpu.make_async_copy(
            slots_ref.at[part], out_ref.at[:, part * step : (part + 1) * step], sems.at[part]
        )

    for part in range(count):
        rows = rows_ref[part * blocks : (part + 1) * blocks].reshape(step, policy)
        slots_ref[part] = lax.dot_general(
            dlogits_ref[...], rows, nt_dims, preferred_element_type=f32
        ).astype(bf16)
        send(part).start()
    for part in range(count):
        send(part).wait()


def copies_kernel(rows_ref, out_ref):
    for other in range(out_ref.shape[0]):
        out_ref[other] = rows_ref[...]


def line_sum_kernel(parts_ref, out_ref):
    out_ref[...] = jnp.sum(parts_ref[...].astype(f32), axis=0).astype(bf16)


def spread_kernel(parts_ref, picks_ref, out_ref):
    total = jnp.sum(parts_ref[...].astype(f32), axis=0).astype(bf16)
    for z in range(out_ref.shape[0]):
        rows = jnp.dot(total, picks_ref[z], preferred_element_type=f32)
        out_ref[z] = fold(rows, jnp.zeros((32, 32), f32)).astype(bf16)


def sum_kernel(parts_ref, out_ref):
    out_ref[...] = unfold(jnp.sum(parts_ref[...].astype(f32), axis=0)).astype(bf16)


def shape(*dims, dtype=bf16):
    return jax.ShapeDtypeStruct(dims, dtype)


def along_lines(blocks, first):
    def device(x, y, c):
        return (x * side + y) * 2 + c

    near, far = (1, 0) if first else (0, 1)
    y_core, x_core = 1 - near, 1 - far
    groups = [[device(x, y, y_core) for y in range(side)] for x in range(side)]
    groups += [[device(x, y, x_core) for x in range(side)] for y in range(side)]
    return lax.all_to_all(blocks, ("x", "y", "c"), 0, 0, axis_index_groups=groups)


def cost(flops, nbytes):
    return pl.CostEstimate(flops=flops, bytes_accessed=nbytes, transcendentals=0)


def body(hidden, head_weight, targets, advantage, policy_mask):
    n_dp = lax.axis_size("z")
    n_plane = lax.axis_size("x") * lax.axis_size("y")
    weight = head_weight.T
    depth = weight.shape[1]
    half = depth // 2
    swap = [(0, 1), (1, 0)]
    local = pl.BlockSpec(memory_space=pltpu.VMEM)

    packed = pl.pallas_call(
        pack_kernel,
        out_shape=shape(n_dp, 128, 128),
        compiler_params=large,
        name="pack",
    )(hidden.T, targets[None], advantage[None], policy_mask[None])
    packed, weight = lax.optimization_barrier((packed, weight))
    packed = lax.all_to_all(packed, "z", 0, 0)
    weight_own, weight_sent = pl.pallas_call(
        prepare_kernel,
        grid=(2,),
        in_specs=[pl.BlockSpec((cols, depth // 2), lambda i: (0, i))],
        out_specs=[pl.BlockSpec((cols, half // 2), lambda i: (0, i))] * 2,
        out_shape=(shape(cols, half), shape(cols, half)),
        compiler_params=large,
        cost_estimate=cost(0, 24_000_000),
        name="prepare",
    )(weight)
    packed, weight_own, weight_sent = lax.optimization_barrier((packed, weight_own, weight_sent))
    rows, meta, picks = pl.pallas_call(
        compact_kernel,
        out_shape=(
            shape(side, width, policy),
            shape(meta_rows, policy, dtype=f32),
            shape(n_dp, policy, tok),
        ),
        compiler_params=small,
        name="compact",
    )(packed)
    rows, weight_sent = lax.optimization_barrier((rows, weight_sent))
    weight_got = lax.ppermute(weight_sent, "c", swap)
    line = along_lines(rows, True)
    lines = pl.pallas_call(
        copies_kernel,
        out_shape=shape(side, side, width, policy),
        compiler_params=small,
        name="copies",
    )(line)
    mine = along_lines(lines, False).reshape(n_plane, width, policy)

    def partial_logits(name, half_weight):
        return pl.pallas_call(
            partial_kernel,
            in_specs=[local] * 2,
            out_shape=shape(cols, policy, dtype=f32),
            compiler_params=small,
            cost_estimate=cost(cols * depth * policy, 6_000_000),
            name=name,
        )(half_weight, mine)

    sent = partial_logits("partial_sent", weight_got)
    got = lax.ppermute(sent, "c", swap)
    own = partial_logits("partial_own", weight_own)
    got, own, rows_sent = lax.optimization_barrier((got, own, mine))
    partner = lax.ppermute(rows_sent, "c", swap)
    logits, stats = pl.pallas_call(
        stats_kernel,
        in_specs=[local] * 3,
        out_shape=(
            shape(cols, policy, dtype=f32),
            shape(2 * n_dp, 4, policy, dtype=f32),
        ),
        compiler_params=small,
        name="stats",
    )(own, got, meta)
    logits_got = lax.ppermute(logits, "c", swap)

    stats = lax.all_to_all(stats, ("z", "c"), 0, 0)
    stats = pl.pallas_call(
        combine_kernel,
        out_shape=shape(n_plane, 4, policy, dtype=f32),
        compiler_params=small,
        name="combine",
    )(stats)
    stats = lax.all_to_all(stats, ("x", "y"), 0, 0)
    stats, partner, logits_got = lax.optimization_barrier((stats, partner, logits_got))

    summed, dlogits, loss = pl.pallas_call(
        grad_kernel,
        in_specs=[local] * 6,
        out_shape=(
            shape(n_plane, width, policy),
            shape(cols, policy),
            shape(1, 1, dtype=f32),
        ),
        compiler_params=small,
        cost_estimate=cost(2 * cols * depth * policy, 12_000_000),
        name="grad",
    )(stats, meta, logits, logits_got, weight_own, weight_got)
    parts = along_lines(summed.reshape(side, side, width, policy), False)
    line = pl.pallas_call(
        line_sum_kernel,
        out_shape=shape(side, width, policy),
        compiler_params=small,
        name="line_sum",
    )(parts)
    parts = along_lines(line, True)
    spread = pl.pallas_call(
        spread_kernel, out_shape=shape(n_dp, 128, 128), compiler_params=small, name="spread"
    )(parts, picks)
    spread, dlogits = lax.optimization_barrier((spread, dlogits))
    parts = lax.all_to_all(spread, "z", 0, 0)
    head_grad = pl.pallas_call(
        head_kernel,
        in_specs=[local] * 3,
        out_specs=pl.BlockSpec(memory_space=pl.ANY),
        out_shape=shape(cols, depth),
        scratch_shapes=[
            pltpu.VMEM((n_plane, 2, width, policy), bf16),
            pltpu.VMEM((4, cols, depth // 4), bf16),
            pltpu.SemaphoreType.DMA((4,)),
        ],
        compiler_params=large,
        cost_estimate=cost(2 * cols * depth * policy, 10_000_000),
        name="head",
    )(dlogits, mine, partner)
    parts, head_grad = lax.optimization_barrier((parts, head_grad))
    grad_rows = pl.pallas_call(
        sum_kernel, out_shape=shape(width, tok), compiler_params=small, name="total"
    )(parts)
    return grad_rows.T, head_grad.T, loss[0, 0]


def solution(mesh):
    fine = Mesh(mesh.devices.reshape(8, 4, 4, 2), ("z", "x", "y", "c"))
    every = ("z", "x", "y", "c")
    in_specs = (P("z", ("x", "y", "c")), P(None, every), P("z"), P("z"), P("z"))
    out_specs = (P("z", ("x", "y", "c")), P(None, every), P())
    return jax.shard_map(body, mesh=fine, in_specs=in_specs, out_specs=out_specs, check_vma=False)
```

```python
import jax
import jax.numpy as jnp
from jax import lax
from jax.experimental import pallas as pl
from jax.experimental.pallas import tpu as pltpu
from jax.sharding import Mesh, PartitionSpec as P

entropy_coef = 0.02
tok = 96
policy = 384
width = 160
cols = 592
side = 4
meta_rows = 16
bf16 = jnp.bfloat16
f32 = jnp.float32
nt_dims = (((1,), (1,)), ((), ()))
tn_dims = (((0,), (0,)), ((), ()))
small = pltpu.CompilerParams(vmem_limit_bytes=20 * 1024 * 1024)
large = pltpu.CompilerParams(vmem_limit_bytes=60 * 1024 * 1024)


def fold(block, corner):
    rest = [block[128:, at : at + 32] for at in (0, 32, 64)]
    return jnp.concatenate([block[:128], jnp.concatenate(rest + [corner], axis=0)], axis=1)


def unfold(folded):
    rest = [folded[at : at + 32, tok:] for at in (0, 32, 64)]
    return jnp.concatenate([folded[:, :tok], jnp.concatenate(rest, axis=1)], axis=0)


def pack_kernel(hidden_ref, targets_ref, adv_ref, mask_ref, out_ref):
    adv = adv_ref[...]
    high = adv.astype(bf16).astype(f32)
    rest = adv - high
    mid = rest.astype(bf16).astype(f32)
    low = rest - mid
    targets = targets_ref[...]
    rows = [
        jnp.where(mask_ref[...] > 0, 1.0, 0.0),
        high,
        mid,
        low,
        (targets & 63).astype(f32),
        ((targets >> 6) & 63).astype(f32),
        (targets >> 12).astype(f32),
    ]
    rows.append(jnp.zeros((1, tok), f32))
    meta = jnp.concatenate(rows, axis=0)
    pieces = [meta[:, at : at + 32] for at in (0, 32, 64)] + [jnp.zeros((8, 32), f32)]
    meta = jnp.concatenate(pieces, axis=0).astype(bf16)
    packed = fold(hidden_ref[...], meta)
    for z in range(out_ref.shape[0]):
        out_ref[z] = packed


def compact_kernel(blocks_ref, rows_ref, meta_ref, picks_ref):
    groups = blocks_ref.shape[0]
    metas = []
    for z in range(groups):
        corner = blocks_ref[z, 96:, :].astype(f32)[:, tok:]
        metas.append(jnp.concatenate([corner[at : at + 8] for at in (0, 8, 16)], axis=1))
    mask = jnp.concatenate([meta[:1] for meta in metas], axis=0)
    before = lax.broadcasted_iota(jnp.int32, (tok, tok), 0) < lax.broadcasted_iota(jnp.int32, (tok, tok), 1)
    prefix = jnp.dot(mask.astype(bf16), before.astype(bf16), preferred_element_type=f32)
    total = jnp.broadcast_to(jnp.sum(mask, axis=1, keepdims=True), mask.shape)
    start = jnp.zeros((1, tok), f32)
    starts = []
    for z in range(groups):
        starts.append(start)
        start = start + total[z : z + 1]
    rank = jnp.where(mask > 0, prefix + jnp.concatenate(starts, axis=0), -1.0).astype(jnp.int32)
    picks_ref[...] = jnp.zeros_like(picks_ref)
    place = lax.broadcasted_iota(jnp.int32, (policy, tok), 0)
    acc = jnp.zeros((width + meta_rows, policy), f32)
    for z in range(groups):
        pick = (place == rank[z : z + 1]).astype(f32).astype(bf16)
        picks_ref[:, z * 128 : z * 128 + tok] = pick
        meta = jnp.concatenate([metas[z], jnp.zeros_like(metas[z])], axis=0).astype(bf16)
        block = jnp.concatenate([unfold(blocks_ref[z]), meta], axis=0)
        acc += lax.dot_general(block, pick, nt_dims, preferred_element_type=f32)
    meta_ref[...] = acc[width:]
    rows = acc[:width].astype(bf16)
    for other in range(rows_ref.shape[0]):
        rows_ref[other] = rows


def core_index():
    return lax.axis_index("c")


def first_column(core):
    line = lax.axis_index("z") * side + lax.axis_index("x")
    return ((line * side + lax.axis_index("y")) * 2 + core) * cols


def place_of(core, block):
    return jnp.where(core == 0, block, block % side * side + block // side)


def meta_target(meta):
    return (meta[4:5] + 64.0 * meta[5:6] + 4096.0 * meta[6:7]).astype(jnp.int32)


def meta_advantage(meta):
    return meta[1:2] + meta[2:3] + meta[3:4]


def column_is_target(first_col, meta):
    column = first_col + lax.broadcasted_iota(jnp.int32, (cols, policy), 0)
    return column == meta_target(meta)


def prepare_kernel(weight_ref, kept_ref, sent_ref):
    for core, (first_ref, second_ref) in enumerate([(kept_ref, sent_ref), (sent_ref, kept_ref)]):

        @pl.when(core_index() == core)
        def _():
            for block in range(kept_ref.shape[1] // width):
                at = slice(block * width, (block + 1) * width)
                first_ref[:, at] = weight_ref[:, 2 * block * width : (2 * block + 1) * width]
                second_ref[:, at] = weight_ref[:, (2 * block + 1) * width : (2 * block + 2) * width]


def partial_kernel(weight_ref, rows_ref, out_ref):
    @pl.when(core_index() == 0)
    def _():
        rows = rows_ref[...].reshape(-1, policy)
        out_ref[...] = jnp.dot(weight_ref[...], rows, preferred_element_type=f32)

    @pl.when(core_index() == 1)
    def _():
        blocks = [rows_ref[k % side * side + k // side] for k in range(rows_ref.shape[0])]
        rows = jnp.concatenate(blocks, axis=0)
        out_ref[...] = jnp.dot(weight_ref[...], rows, preferred_element_type=f32)


def stats_kernel(own_ref, got_ref, meta_ref, logits_ref, stats_ref):
    logits = own_ref[...] + got_ref[...]
    logits_ref[...] = logits
    top = jnp.max(logits, axis=0, keepdims=True)
    shifted = jnp.exp(logits - top)
    total = jnp.sum(shifted, axis=0, keepdims=True)
    mix = jnp.sum(shifted * logits, axis=0, keepdims=True)
    chosen = jnp.sum(
        jnp.where(column_is_target(first_column(core_index()), meta_ref[...]), logits, 0.0), axis=0, keepdims=True
    )
    stats = jnp.concatenate([top, total, mix, chosen], axis=0)
    for other in range(stats_ref.shape[0]):
        stats_ref[other] = stats


def combine(stats):
    tops = stats[:, 0:1, :]
    top = jnp.max(tops, axis=0)
    scale = jnp.exp(tops - top[None])
    total = jnp.sum(stats[:, 1:2, :] * scale, axis=0)
    mix = jnp.sum(stats[:, 2:3, :] * scale, axis=0)
    chosen = jnp.sum(stats[:, 3:4, :], axis=0)
    return top, total, mix, chosen


def combine_kernel(in_ref, out_ref):
    top, total, mix, chosen = combine(in_ref[...])
    stats = jnp.concatenate([top, total, mix, chosen], axis=0)
    for other in range(out_ref.shape[0]):
        out_ref[other] = stats


def grad_kernel(stats_ref, meta_ref, logits_ref, other_ref, weight_ref, weight_got_ref, grad_ref, dlogits_ref, loss_ref
):
    top, total, mix, chosen = combine(stats_ref[...])
    meta = meta_ref[...]
    adv = meta_advantage(meta)
    mean = mix / total
    log_total = top + jnp.log(total)
    loss = jnp.sum(
        adv * (chosen - log_total) + entropy_coef * (log_total - mean), axis=1, keepdims=True
    )
    loss_ref[...] = -loss / policy
    share = 1.0 / (total * policy)
    spread = entropy_coef * share

    def dlogits_of(logits, first_col):
        soft = jnp.exp(logits - top) * (adv * share + spread * (logits - mean))
        hit = jnp.where(column_is_target(first_col, meta), adv / policy, 0.0)
        return (soft - hit).astype(bf16)

    def part(weight, dlogits):
        return lax.dot_general(weight, dlogits, tn_dims, preferred_element_type=f32)

    whole = cols // 256 * 256
    own = dlogits_of(logits_ref[...], first_column(core_index()))
    dlogits_ref[...] = own
    out = part(weight_ref[:whole], own[:whole])
    other = dlogits_of(other_ref[...], first_column(1 - core_index()))
    out += part(weight_got_ref[:whole], other[:whole])
    weight = jnp.concatenate([weight_ref[whole:], weight_got_ref[whole:]], axis=0)
    out += part(weight, jnp.concatenate([own[whole:], other[whole:]], axis=0))
    for block in range(grad_ref.shape[0]):
        rows = out[block * width : (block + 1) * width]
        grad_ref[place_of(core_index(), block)] = rows.astype(bf16)


def head_kernel(dlogits_ref, mine_ref, partner_ref, out_ref, rows_ref, slots_ref, sems):
    for core, (first, second) in enumerate([(mine_ref, partner_ref), (partner_ref, mine_ref)]):

        @pl.when(core_index() == core)
        def _():
            for block in range(first.shape[0]):
                rows_ref[block, 0] = first[block]
                rows_ref[block, 1] = second[block % side * side + block // side]

    count = slots_ref.shape[0]
    step = slots_ref.shape[2]
    blocks = rows_ref.shape[0] // count

    def send(part):
        return pltpu.make_async_copy(
            slots_ref.at[part], out_ref.at[:, part * step : (part + 1) * step], sems.at[part]
        )

    for part in range(count):
        rows = rows_ref[part * blocks : (part + 1) * blocks].reshape(step, policy)
        slots_ref[part] = lax.dot_general(
            dlogits_ref[...], rows, nt_dims, preferred_element_type=f32
        ).astype(bf16)
        send(part).start()
    for part in range(count):
        send(part).wait()


def copies_kernel(rows_ref, out_ref):
    for other in range(out_ref.shape[0]):
        out_ref[other] = rows_ref[...]


def line_sum_kernel(parts_ref, out_ref):
    out_ref[...] = jnp.sum(parts_ref[...].astype(f32), axis=0).astype(bf16)


def spread_kernel(parts_ref, picks_ref, out_ref):
    total = jnp.sum(parts_ref[...].astype(f32), axis=0).astype(bf16)
    rows = jnp.dot(total, picks_ref[...], preferred_element_type=f32)
    for z in range(out_ref.shape[0]):
        at = z * 128
        out_ref[z] = fold(rows[:, at : at + tok], jnp.zeros((32, 32), f32)).astype(bf16)


def sum_kernel(parts_ref, out_ref):
    out_ref[...] = unfold(jnp.sum(parts_ref[...].astype(f32), axis=0)).astype(bf16)


def shape(*dims, dtype=bf16):
    return jax.ShapeDtypeStruct(dims, dtype)


def along_lines(blocks, first):
    def device(x, y, c):
        return (x * side + y) * 2 + c

    near, far = (1, 0) if first else (0, 1)
    y_core, x_core = 1 - near, 1 - far
    groups = [[device(x, y, y_core) for y in range(side)] for x in range(side)]
    groups += [[device(x, y, x_core) for x in range(side)] for y in range(side)]
    return lax.all_to_all(blocks, ("x", "y", "c"), 0, 0, axis_index_groups=groups)


def along_z(blocks):
    planes = list(range(blocks.shape[0]))[::-1]
    return lax.all_to_all(blocks, "z", 0, 0, axis_index_groups=[planes])


def cost(flops, nbytes):
    return pl.CostEstimate(flops=flops, bytes_accessed=nbytes, transcendentals=0)


def body(hidden, head_weight, targets, advantage, policy_mask):
    n_dp = lax.axis_size("z")
    n_plane = lax.axis_size("x") * lax.axis_size("y")
    weight = head_weight.T
    depth = weight.shape[1]
    half = depth // 2
    swap = [(0, 1), (1, 0)]
    local = pl.BlockSpec(memory_space=pltpu.VMEM)

    packed = pl.pallas_call(
        pack_kernel,
        out_shape=shape(n_dp, 128, 128),
        compiler_params=large,
        name="pack",
    )(hidden.T, targets[None], advantage[None], policy_mask[None])
    packed, weight = lax.optimization_barrier((packed, weight))
    packed = along_z(packed)
    weight_own, weight_sent = pl.pallas_call(
        prepare_kernel,
        grid=(2,),
        in_specs=[pl.BlockSpec((cols, depth // 2), lambda i: (0, i))],
        out_specs=[pl.BlockSpec((cols, half // 2), lambda i: (0, i))] * 2,
        out_shape=(shape(cols, half), shape(cols, half)),
        compiler_params=large,
        cost_estimate=cost(0, 24_000_000),
        name="prepare",
    )(weight)
    packed, weight_own, weight_sent = lax.optimization_barrier((packed, weight_own, weight_sent))
    rows, meta, picks = pl.pallas_call(
        compact_kernel,
        out_shape=(
            shape(side, width, policy),
            shape(meta_rows, policy, dtype=f32),
            shape(policy, n_dp * 128),
        ),
        compiler_params=small,
        name="compact",
    )(packed)
    rows, weight_sent = lax.optimization_barrier((rows, weight_sent))
    weight_got = lax.ppermute(weight_sent, "c", swap)
    line = along_lines(rows, True)
    lines = pl.pallas_call(
        copies_kernel,
        out_shape=shape(side, side, width, policy),
        compiler_params=small,
        name="copies",
    )(line)
    mine = along_lines(lines, False).reshape(n_plane, width, policy)

    def partial_logits(name, half_weight):
        return pl.pallas_call(
            partial_kernel,
            in_specs=[local] * 2,
            out_shape=shape(cols, policy, dtype=f32),
            compiler_params=small,
            cost_estimate=cost(cols * depth * policy, 6_000_000),
            name=name,
        )(half_weight, mine)

    sent = partial_logits("partial_sent", weight_got)
    got = lax.ppermute(sent, "c", swap)
    own = partial_logits("partial_own", weight_own)
    got, own, rows_sent = lax.optimization_barrier((got, own, mine))
    partner = lax.ppermute(rows_sent, "c", swap)
    logits, stats = pl.pallas_call(
        stats_kernel,
        in_specs=[local] * 3,
        out_shape=(
            shape(cols, policy, dtype=f32),
            shape(2 * n_dp, 4, policy, dtype=f32),
        ),
        compiler_params=small,
        name="stats",
    )(own, got, meta)
    logits_got = lax.ppermute(logits, "c", swap)

    stats = lax.all_to_all(stats, ("z", "c"), 0, 0)
    stats = pl.pallas_call(
        combine_kernel,
        out_shape=shape(n_plane, 4, policy, dtype=f32),
        compiler_params=small,
        name="combine",
    )(stats)
    stats = lax.all_to_all(stats, ("x", "y"), 0, 0)
    stats, partner, logits_got = lax.optimization_barrier((stats, partner, logits_got))

    summed, dlogits, loss = pl.pallas_call(
        grad_kernel,
        in_specs=[local] * 6,
        out_shape=(
            shape(n_plane, width, policy),
            shape(cols, policy),
            shape(1, 1, dtype=f32),
        ),
        compiler_params=small,
        cost_estimate=cost(2 * cols * depth * policy, 12_000_000),
        name="grad",
    )(stats, meta, logits, logits_got, weight_own, weight_got)
    parts = along_lines(summed.reshape(side, side, width, policy), False)
    line = pl.pallas_call(
        line_sum_kernel,
        out_shape=shape(side, width, policy),
        compiler_params=small,
        name="line_sum",
    )(parts)
    parts = along_lines(line, True)
    spread = pl.pallas_call(
        spread_kernel, out_shape=shape(n_dp, 128, 128), compiler_params=small, name="spread"
    )(parts, picks)
    spread, dlogits = lax.optimization_barrier((spread, dlogits))
    parts = along_z(spread)
    head_grad = pl.pallas_call(
        head_kernel,
        in_specs=[local] * 3,
        out_specs=pl.BlockSpec(memory_space=pl.ANY),
        out_shape=shape(cols, depth),
        scratch_shapes=[
            pltpu.VMEM((n_plane, 2, width, policy), bf16),
            pltpu.VMEM((4, cols, depth // 4), bf16),
            pltpu.SemaphoreType.DMA((4,)),
        ],
        compiler_params=large,
        cost_estimate=cost(2 * cols * depth * policy, 10_000_000),
        name="head",
    )(dlogits, mine, partner)
    parts, head_grad = lax.optimization_barrier((parts, head_grad))
    grad_rows = pl.pallas_call(
        sum_kernel, out_shape=shape(width, tok), compiler_params=small, name="total"
    )(parts)
    return grad_rows.T, head_grad.T, loss[0, 0]


def solution(mesh):
    fine = Mesh(mesh.devices.reshape(8, 4, 4, 2), ("z", "x", "y", "c"))
    every = ("z", "x", "y", "c")
    in_specs = (P("z", ("x", "y", "c")), P(None, every), P("z"), P("z"), P("z"))
    out_specs = (P("z", ("x", "y", "c")), P(None, every), P())
    return jax.shard_map(body, mesh=fine, in_specs=in_specs, out_specs=out_specs, check_vma=False)
```

```python
import jax
import jax.numpy as jnp
from jax import lax
from jax.experimental import pallas as pl
from jax.experimental.pallas import tpu as pltpu
from jax.sharding import Mesh, PartitionSpec as P

entropy_coef = 0.02
tok = 96
policy = 384
width = 160
cols = 592
side = 4
meta_rows = 16
bf16 = jnp.bfloat16
f32 = jnp.float32
nt_dims = (((1,), (1,)), ((), ()))
tn_dims = (((0,), (0,)), ((), ()))
small = pltpu.CompilerParams(vmem_limit_bytes=20 * 1024 * 1024)
large = pltpu.CompilerParams(vmem_limit_bytes=60 * 1024 * 1024)


def fold(block, corner):
    rest = [block[128:, at : at + 32] for at in (0, 32, 64)]
    return jnp.concatenate([block[:128], jnp.concatenate(rest + [corner], axis=0)], axis=1)


def unfold(folded):
    rest = [folded[at : at + 32, tok:] for at in (0, 32, 64)]
    return jnp.concatenate([folded[:, :tok], jnp.concatenate(rest, axis=1)], axis=0)


def pack_kernel(hidden_ref, targets_ref, adv_ref, mask_ref, out_ref):
    adv = adv_ref[...]
    high = adv.astype(bf16).astype(f32)
    rest = adv - high
    mid = rest.astype(bf16).astype(f32)
    low = rest - mid
    targets = targets_ref[...]
    rows = [
        jnp.where(mask_ref[...] > 0, 1.0, 0.0),
        high,
        mid,
        low,
        (targets & 63).astype(f32),
        ((targets >> 6) & 63).astype(f32),
        (targets >> 12).astype(f32),
    ]
    rows.append(jnp.zeros((1, tok), f32))
    meta = jnp.concatenate(rows, axis=0)
    pieces = [meta[:, at : at + 32] for at in (0, 32, 64)] + [jnp.zeros((8, 32), f32)]
    meta = jnp.concatenate(pieces, axis=0).astype(bf16)
    packed = fold(hidden_ref[...], meta)
    for z in range(out_ref.shape[0]):
        out_ref[z] = packed


def compact_kernel(blocks_ref, rows_ref, meta_ref, picks_ref):
    groups = blocks_ref.shape[0]
    metas = []
    for z in range(groups):
        corner = blocks_ref[z, 96:, :].astype(f32)[:, tok:]
        metas.append(jnp.concatenate([corner[at : at + 8] for at in (0, 8, 16)], axis=1))
    mask = jnp.concatenate([meta[:1] for meta in metas], axis=0)
    before = lax.broadcasted_iota(jnp.int32, (tok, tok), 0) < lax.broadcasted_iota(jnp.int32, (tok, tok), 1)
    prefix = jnp.dot(mask.astype(bf16), before.astype(bf16), preferred_element_type=f32)
    total = jnp.broadcast_to(jnp.sum(mask, axis=1, keepdims=True), mask.shape)
    start = jnp.zeros((1, tok), f32)
    starts = []
    for z in range(groups):
        starts.append(start)
        start = start + total[z : z + 1]
    rank = jnp.where(mask > 0, prefix + jnp.concatenate(starts, axis=0), -1.0).astype(jnp.int32)
    picks_ref[...] = jnp.zeros_like(picks_ref)
    place = lax.broadcasted_iota(jnp.int32, (policy, tok), 0)
    acc = jnp.zeros((width + meta_rows, policy), f32)
    for z in range(groups):
        pick = (place == rank[z : z + 1]).astype(f32).astype(bf16)
        picks_ref[:, z * 128 : z * 128 + tok] = pick
        meta = jnp.concatenate([metas[z], jnp.zeros_like(metas[z])], axis=0).astype(bf16)
        block = jnp.concatenate([unfold(blocks_ref[z]), meta], axis=0)
        acc += lax.dot_general(block, pick, nt_dims, preferred_element_type=f32)
    meta_ref[...] = acc[width:]
    rows = acc[:width].astype(bf16)
    for other in range(rows_ref.shape[0]):
        rows_ref[other] = rows


def core_index():
    return lax.axis_index("c")


def first_column(core):
    line = lax.axis_index("z") * side + lax.axis_index("x")
    return ((line * side + lax.axis_index("y")) * 2 + core) * cols


def place_of(core, block):
    return jnp.where(core == 0, block, block % side * side + block // side)


def meta_target(meta):
    return (meta[4:5] + 64.0 * meta[5:6] + 4096.0 * meta[6:7]).astype(jnp.int32)


def meta_advantage(meta):
    return meta[1:2] + meta[2:3] + meta[3:4]


def column_is_target(first_col, meta):
    column = first_col + lax.broadcasted_iota(jnp.int32, (cols, policy), 0)
    return column == meta_target(meta)


def prepare_kernel(weight_ref, kept_ref, sent_ref):
    for core, (first_ref, second_ref) in enumerate([(kept_ref, sent_ref), (sent_ref, kept_ref)]):

        @pl.when(core_index() == core)
        def _():
            for block in range(kept_ref.shape[1] // width):
                at = slice(block * width, (block + 1) * width)
                first_ref[:, at] = weight_ref[:, 2 * block * width : (2 * block + 1) * width]
                second_ref[:, at] = weight_ref[:, (2 * block + 1) * width : (2 * block + 2) * width]


def partial_kernel(weight_ref, rows_ref, out_ref):
    @pl.when(core_index() == 0)
    def _():
        rows = rows_ref[...].reshape(-1, policy)
        out_ref[...] = jnp.dot(weight_ref[...], rows, preferred_element_type=f32)

    @pl.when(core_index() == 1)
    def _():
        blocks = [rows_ref[k % side * side + k // side] for k in range(rows_ref.shape[0])]
        rows = jnp.concatenate(blocks, axis=0)
        out_ref[...] = jnp.dot(weight_ref[...], rows, preferred_element_type=f32)


def stats_kernel(own_ref, got_ref, meta_ref, logits_ref, stats_ref):
    logits = own_ref[...] + got_ref[...]
    logits_ref[...] = logits
    top = jnp.max(logits, axis=0, keepdims=True)
    shifted = jnp.exp(logits - top)
    total = jnp.sum(shifted, axis=0, keepdims=True)
    mix = jnp.sum(shifted * logits, axis=0, keepdims=True)
    chosen = jnp.sum(
        jnp.where(column_is_target(first_column(core_index()), meta_ref[...]), logits, 0.0), axis=0, keepdims=True
    )
    stats = jnp.concatenate([top, total, mix, chosen], axis=0)
    for other in range(stats_ref.shape[0]):
        stats_ref[other] = stats


def combine(stats):
    tops = stats[:, 0:1, :]
    top = jnp.max(tops, axis=0)
    scale = jnp.exp(tops - top[None])
    total = jnp.sum(stats[:, 1:2, :] * scale, axis=0)
    mix = jnp.sum(stats[:, 2:3, :] * scale, axis=0)
    chosen = jnp.sum(stats[:, 3:4, :], axis=0)
    return top, total, mix, chosen


def combine_kernel(in_ref, out_ref):
    top, total, mix, chosen = combine(in_ref[...])
    stats = jnp.concatenate([top, total, mix, chosen], axis=0)
    for other in range(out_ref.shape[0]):
        out_ref[other] = stats


def grad_kernel(stats_ref, meta_ref, logits_ref, other_ref, weight_ref, weight_got_ref, grad_ref, dlogits_ref, loss_ref
):
    top, total, mix, chosen = combine(stats_ref[...])
    meta = meta_ref[...]
    adv = meta_advantage(meta)
    mean = mix / total
    log_total = top + jnp.log(total)
    loss = jnp.sum(
        adv * (chosen - log_total) + entropy_coef * (log_total - mean), axis=1, keepdims=True
    )
    loss_ref[...] = -loss / policy
    share = 1.0 / (total * policy)
    spread = entropy_coef * share

    def dlogits_of(logits, first_col):
        soft = jnp.exp(logits - top) * (adv * share + spread * (logits - mean))
        hit = jnp.where(column_is_target(first_col, meta), adv / policy, 0.0)
        return (soft - hit).astype(bf16)

    def part(weight, dlogits):
        return lax.dot_general(weight, dlogits, tn_dims, preferred_element_type=f32)

    whole = cols // 256 * 256
    own = dlogits_of(logits_ref[...], first_column(core_index()))
    dlogits_ref[...] = own
    out = part(weight_ref[:whole], own[:whole])
    other = dlogits_of(other_ref[...], first_column(1 - core_index()))
    out += part(weight_got_ref[:whole], other[:whole])
    weight = jnp.concatenate([weight_ref[whole:], weight_got_ref[whole:]], axis=0)
    out += part(weight, jnp.concatenate([own[whole:], other[whole:]], axis=0))
    for block in range(grad_ref.shape[0]):
        rows = out[block * width : (block + 1) * width]
        grad_ref[place_of(core_index(), block)] = rows.astype(bf16)


def head_kernel(dlogits_ref, mine_ref, partner_ref, out_ref, rows_ref, slots_ref, sems):
    for core, (first, second) in enumerate([(mine_ref, partner_ref), (partner_ref, mine_ref)]):

        @pl.when(core_index() == core)
        def _():
            for block in range(first.shape[0]):
                rows_ref[block, 0] = first[block]
                rows_ref[block, 1] = second[block % side * side + block // side]

    count = slots_ref.shape[0]
    step = slots_ref.shape[2]
    blocks = rows_ref.shape[0] // count

    def send(part):
        return pltpu.make_async_copy(
            slots_ref.at[part], out_ref.at[:, part * step : (part + 1) * step], sems.at[part]
        )

    for part in range(count):
        rows = rows_ref[part * blocks : (part + 1) * blocks].reshape(step, policy)
        slots_ref[part] = lax.dot_general(
            dlogits_ref[...], rows, nt_dims, preferred_element_type=f32
        ).astype(bf16)
        send(part).start()
    for part in range(count):
        send(part).wait()


def copies_kernel(rows_ref, out_ref):
    for other in range(out_ref.shape[0]):
        out_ref[other] = rows_ref[...]


def line_sum_kernel(parts_ref, out_ref):
    out_ref[...] = jnp.sum(parts_ref[...].astype(f32), axis=0).astype(bf16)


def spread_kernel(parts_ref, picks_ref, out_ref):
    total = jnp.sum(parts_ref[...].astype(f32), axis=0).astype(bf16)
    rows = jnp.dot(total, picks_ref[...], preferred_element_type=f32)
    for z in range(out_ref.shape[0]):
        at = z * 128
        out_ref[z] = fold(rows[:, at : at + tok], jnp.zeros((32, 32), f32)).astype(bf16)


def sum_kernel(parts_ref, out_ref):
    out_ref[...] = unfold(jnp.sum(parts_ref[...].astype(f32), axis=0)).astype(bf16)


def shape(*dims, dtype=bf16):
    return jax.ShapeDtypeStruct(dims, dtype)


def along_lines(blocks, first):
    def device(x, y, c):
        return (x * side + y) * 2 + c

    near, far = (1, 0) if first else (0, 1)
    y_core, x_core = 1 - near, 1 - far
    groups = [[device(x, y, y_core) for y in range(side)] for x in range(side)]
    groups += [[device(x, y, x_core) for x in range(side)] for y in range(side)]
    return lax.all_to_all(blocks, ("x", "y", "c"), 0, 0, axis_index_groups=groups)


def along_z(blocks):
    planes = list(range(blocks.shape[0]))[::-1]
    return lax.all_to_all(blocks, "z", 0, 0, axis_index_groups=[planes])


def cost(flops, nbytes):
    return pl.CostEstimate(flops=flops, bytes_accessed=nbytes, transcendentals=0)


def body(hidden, head_weight, targets, advantage, policy_mask):
    n_dp = lax.axis_size("z")
    n_plane = lax.axis_size("x") * lax.axis_size("y")
    weight = head_weight.T
    depth = weight.shape[1]
    half = depth // 2
    swap = [(0, 1), (1, 0)]
    local = pl.BlockSpec(memory_space=pltpu.VMEM)

    packed = pl.pallas_call(
        pack_kernel,
        out_shape=shape(n_dp, 128, 128),
        compiler_params=large,
        name="pack",
    )(hidden.T, targets[None], advantage[None], policy_mask[None])
    packed, weight = lax.optimization_barrier((packed, weight))
    packed = along_z(packed)
    weight_own, weight_sent = pl.pallas_call(
        prepare_kernel,
        grid=(2,),
        in_specs=[pl.BlockSpec((cols, depth // 2), lambda i: (0, i))],
        out_specs=[pl.BlockSpec((cols, half // 2), lambda i: (0, i))] * 2,
        out_shape=(shape(cols, half), shape(cols, half)),
        compiler_params=large,
        cost_estimate=cost(0, 24_000_000),
        name="prepare",
    )(weight)
    packed, weight_own, weight_sent = lax.optimization_barrier((packed, weight_own, weight_sent))
    rows, meta, picks = pl.pallas_call(
        compact_kernel,
        out_shape=(
            shape(side, width, policy),
            shape(meta_rows, policy, dtype=f32),
            shape(policy, n_dp * 128),
        ),
        compiler_params=small,
        name="compact",
    )(packed)
    rows, weight_sent = lax.optimization_barrier((rows, weight_sent))
    weight_got = lax.ppermute(weight_sent, "c", swap)
    line = along_lines(rows, True)
    lines = pl.pallas_call(
        copies_kernel,
        out_shape=shape(side, side, width, policy),
        compiler_params=small,
        name="copies",
    )(line)
    mine = along_lines(lines, False).reshape(n_plane, width, policy)

    def partial_logits(name, half_weight):
        return pl.pallas_call(
            partial_kernel,
            in_specs=[local] * 2,
            out_shape=shape(cols, policy, dtype=f32),
            compiler_params=small,
            cost_estimate=cost(cols * depth * policy, 6_000_000),
            name=name,
        )(half_weight, mine)

    sent = partial_logits("partial_sent", weight_got)
    got = lax.ppermute(sent, "c", swap)
    own = partial_logits("partial_own", weight_own)
    got, own, rows_sent = lax.optimization_barrier((got, own, mine))
    partner = lax.ppermute(rows_sent, "c", swap)
    logits, stats = pl.pallas_call(
        stats_kernel,
        in_specs=[local] * 3,
        out_shape=(
            shape(cols, policy, dtype=f32),
            shape(2 * n_dp, 4, policy, dtype=f32),
        ),
        compiler_params=small,
        name="stats",
    )(own, got, meta)
    logits_got = lax.ppermute(logits, "c", swap)

    falling = list(range(2 * n_dp))[::-1]
    stats = lax.all_to_all(stats, ("z", "c"), 0, 0, axis_index_groups=[falling])
    stats = pl.pallas_call(
        combine_kernel,
        out_shape=shape(n_plane, 4, policy, dtype=f32),
        compiler_params=small,
        name="combine",
    )(stats)
    stats = lax.all_to_all(stats, ("x", "y"), 0, 0)
    stats, partner, logits_got = lax.optimization_barrier((stats, partner, logits_got))

    summed, dlogits, loss = pl.pallas_call(
        grad_kernel,
        in_specs=[local] * 6,
        out_shape=(
            shape(n_plane, width, policy),
            shape(cols, policy),
            shape(1, 1, dtype=f32),
        ),
        compiler_params=small,
        cost_estimate=cost(2 * cols * depth * policy, 12_000_000),
        name="grad",
    )(stats, meta, logits, logits_got, weight_own, weight_got)
    parts = along_lines(summed.reshape(side, side, width, policy), False)
    line = pl.pallas_call(
        line_sum_kernel,
        out_shape=shape(side, width, policy),
        compiler_params=small,
        name="line_sum",
    )(parts)
    parts = along_lines(line, True)
    spread = pl.pallas_call(
        spread_kernel, out_shape=shape(n_dp, 128, 128), compiler_params=small, name="spread"
    )(parts, picks)
    spread, dlogits = lax.optimization_barrier((spread, dlogits))
    parts = along_z(spread)
    head_grad = pl.pallas_call(
        head_kernel,
        in_specs=[local] * 3,
        out_specs=pl.BlockSpec(memory_space=pl.ANY),
        out_shape=shape(cols, depth),
        scratch_shapes=[
            pltpu.VMEM((n_plane, 2, width, policy), bf16),
            pltpu.VMEM((4, cols, depth // 4), bf16),
            pltpu.SemaphoreType.DMA((4,)),
        ],
        compiler_params=large,
        cost_estimate=cost(2 * cols * depth * policy, 10_000_000),
        name="head",
    )(dlogits, mine, partner)
    parts, head_grad = lax.optimization_barrier((parts, head_grad))
    grad_rows = pl.pallas_call(
        sum_kernel, out_shape=shape(width, tok), compiler_params=small, name="total"
    )(parts)
    return grad_rows.T, head_grad.T, loss[0, 0]


def solution(mesh):
    fine = Mesh(mesh.devices.reshape(8, 4, 4, 2), ("z", "x", "y", "c"))
    every = ("z", "x", "y", "c")
    in_specs = (P("z", ("x", "y", "c")), P(None, every), P("z"), P("z"), P("z"))
    out_specs = (P("z", ("x", "y", "c")), P(None, every), P())
    return jax.shard_map(body, mesh=fine, in_specs=in_specs, out_specs=out_specs, check_vma=False)
```
